32 devices in a mesh: dp: 8 (over y, x, core), mp: 4 (over z).
Axes of the slice: x: 2, y: 2, z: 4, core: 2. Of those that a mesh axis runs over, the one named last changes fastest.
Arguments:
- inputs: bfloat16 [8192, 2048], P('dp', 'mp'), may hold values from -6 to 6
- segment_ids: int32 [8, 1024], P('dp'), may hold values from 0 to 3, never falling along the last dimension, each value on 1 to 512 neighbouring positions
- width_bucket: int32 [8, 1024], P('dp'), may hold values from 0 to 3, as said below
- attn_gain: float32 [2048], P('mp'), may hold values from 0.25 to 1.75
- attn_bias: float32 [2048], P('mp'), may hold values from -1.5 to 1.5
- qkv_weight: bfloat16 [3, 2048, 2048], P(None, None, 'mp'), may hold values from -0.125 to 0.125
- proj_weight: bfloat16 [2048, 2048], P('mp'), may hold values from -0.75 to 0.75
- ffn_gain: float32 [2048], P('mp'), may hold values from 0.25 to 1.75
- ffn_bias: float32 [2048], P('mp'), may hold values from -1.5 to 1.5
- up_weight: bfloat16 [2048, 8192], P(None, 'mp'), may hold values from -0.125 to 0.125
- down_weight: bfloat16 [8192, 2048], P('mp'), may hold values from -0.0625 to 0.0625
- grad_result: bfloat16 [8192, 2048], P('dp', 'mp'), may hold values from -6 to 6
Outputs:
- block_output: bfloat16 [8192, 2048], P('dp', 'mp')
- grad_input: float32 [8192, 2048], P('dp', 'mp')
- grad_attn_gain: float32 [2048], P('mp')
- grad_attn_bias: float32 [2048], P('mp')
- grad_qkv: float32 [3, 2048, 2048], P(None, None, 'mp')
- grad_proj: float32 [2048, 2048], P('mp')
- grad_ffn_gain: float32 [2048], P('mp')
- grad_ffn_bias: float32 [2048], P('mp')
- grad_up: float32 [2048, 8192], P(None, 'mp')
- grad_down: float32 [8192, 2048], P('mp')
The draws below stay inside these ranges and needn't reach their ends.
Inputs may be any that keep to these rules, and one draw needn't show every extreme that they name: `segment_ids`: in each row the document numbers never fall and all 4 documents appear; the longest holds exactly 512 tokens. `width_bucket`: each packed row holds exactly 256 tokens of each of the four buckets, in any order.
All inputs are finite; a program needn't handle non-finite values.
Results may differ from the reference program's by a relative error of at most 0.014.
Values may be sent and summed in bfloat16 or wider, within the bound.
No kernel may reach another device: no remote copies, remote signals or barrier semaphores. Data moves between devices by JAX's collectives and lax.ppermute only.
A program may use at most 256 MiB of HBM per device.

```python
import math
import jax
import jax.numpy as jnp
import numpy as np
from jax import lax

D = 2048
HEADS = 16
HEAD_DIM = 128
FF = 8192
ROW = 1024
DOCS = 4
ROWS = 8
TOKENS = 8192


def draw_width_bucket(key, part):
    key = jax.random.fold_in(key, 11)
    base = jnp.arange(ROW, dtype=jnp.int32) * 4 // ROW
    row_keys = jax.random.split(key, ROWS)
    return jax.vmap(lambda row_key: jax.random.permutation(row_key, base))(row_keys).astype(jnp.int32)


def block_scale(rng, dims, shards, least, largest):
    loudness, own = 1.0, jax.random.fold_in(rng, 6)
    for position, parts in shards:
        steps = jnp.exp(jax.random.uniform(jax.random.fold_in(own, position), (parts,), jnp.float32, least / len(shards), largest / len(shards)))
        loudness = loudness * jnp.repeat(steps, dims[position] // parts).reshape([-1 if axis == position else 1 for axis in range(len(dims))])
    return loudness


def split_up(amount, total, most, skew):
    portions = [(1 << 20) // math.isqrt(rank ** skew) + 1 for rank in range(2, amount + 1)]
    surplus, holding = total - most - (amount - 1), [1] * (amount - 1)
    while surplus > 0:
        free = [i for i in range(amount - 1) if holding[i] < most]
        pool, budget = sum([portions[i] for i in free]), surplus
        for i in free:
            more = min(most - holding[i], max(1, budget * portions[i] // pool), surplus)
            holding[i] = holding[i] + more
            surplus = surplus - more
    return np.array([most] + holding)


def ragged_sizes(stream_key, number_of, total, bound, slope):
    if number_of == 2:
        one = jax.random.randint(stream_key, (), max(1, total - bound), min(bound, total - 1) + 1)
        return jnp.stack([one, total - one])
    sizes = jnp.asarray(split_up(number_of, total, bound, slope), jnp.int32)
    couples = (number_of - 1) // 2
    source_of, taker = sizes[1:1 + 2 * couples:2], sizes[2:2 + 2 * couples:2]
    margin = jnp.minimum(source_of - 1, bound - taker)
    shifted = jax.random.randint(jax.random.fold_in(stream_key, 1), (couples,), 0, 1 << 20) % (margin + 1)
    sizes = sizes.at[1:1 + 2 * couples:2].set(source_of - shifted).at[2:2 + 2 * couples:2].set(taker + shifted)
    return sizes[jax.random.permutation(jax.random.fold_in(stream_key, 2), number_of)]


def scatter_about(own_key, shape, spread, reach, shards=(), held_as=jnp.bfloat16):
    array = jax.random.normal(own_key, shape, jnp.float32) * spread
    if len(shards) > 0:
        array = block_scale(own_key, shape, shards, -0.22, 0.18) * array
    return jnp.clip(array, min=-reach, max=reach).astype(held_as)


def setup_inputs(seed: int = 0) -> dict:
    splits = jax.random.split(jax.random.key(seed), 13)
    inputs = scatter_about(splits[0], (TOKENS, D), 1.0, 6.0, ((0, 8), (1, 4)))
    segment_ids = jax.vmap(lambda own: jnp.searchsorted(jnp.cumsum(ragged_sizes(own, DOCS, ROW, ROW // 2, 2)), jnp.arange(ROW), side="right"))(jax.random.split(splits[1], ROWS)).reshape((ROWS, ROW)).astype(jnp.int32)
    width_bucket = draw_width_bucket(jax.random.fold_in(splits[12], 71), 0)
    attn_gain = jnp.clip(1.0 + 0.15 * jax.random.normal(splits[3], (D,), jnp.float32), 0.25, 1.75)
    attn_bias = scatter_about(splits[4], (D,), 0.3, 1.5, ((0, 4),), jnp.float32)
    qkv_weight = scatter_about(splits[5], (3, D, D), D ** -0.5, 0.125, ((2, 4),))
    proj_weight = scatter_about(splits[6], (D, D), (D // 32) ** -0.5, 0.75, ((0, 4),))
    ffn_gain = jnp.clip(1.0 + 0.15 * jax.random.normal(splits[7], (D,), jnp.float32), 0.25, 1.75)
    ffn_bias = scatter_about(splits[8], (D,), 0.3, 1.5, ((0, 4),), jnp.float32)
    up_weight = scatter_about(splits[9], (D, FF), D ** -0.5, 0.125, ((1, 4),))
    down_weight = scatter_about(splits[10], (FF, D), FF ** -0.5, 0.0625, ((0, 4),))
    grad_result = scatter_about(splits[11], (TOKENS, D), 1.0, 6.0, ((0, 8), (1, 4)))
    return {"inputs": inputs, "segment_ids": segment_ids, "width_bucket": width_bucket, "attn_gain": attn_gain, "attn_bias": attn_bias, "qkv_weight": qkv_weight, "proj_weight": proj_weight, "ffn_gain": ffn_gain, "ffn_bias": ffn_bias, "up_weight": up_weight, "down_weight": down_weight, "grad_result": grad_result}


HIGH = lax.Precision.HIGHEST

@jax.custom_vjp
def low(v):
    return lax.optimization_barrier(v.astype(jnp.bfloat16)).astype(jnp.float32)

@jax.custom_vjp
def low_back(v):
    return v

def low_keep(v):
    return (low(v), None)

def low_pass(kept, grad):
    return (grad,)

def back_keep(v):
    return (v, None)

def back_low(kept, grad):
    return (low(grad),)
low.defvjp(low_keep, low_pass)
low_back.defvjp(back_keep, back_low)

def both_ways(value):
    return low_back(low(value))

def normalize(values, gain_vec, bias_vec):
    mean_val = lax.optimization_barrier(jnp.mean(values, axis=-1, keepdims=True))
    centred = values - mean_val
    rstd_val = lax.rsqrt(lax.optimization_barrier(jnp.mean(centred * centred, axis=-1, keepdims=True)) + 1e-05)
    return centred * rstd_val * gain_vec + bias_vec

def rotate(values, cosine, sine_table):
    half_dim = values.shape[-1] // 2
    former = values[..., :half_dim]
    latter = values[..., half_dim:]
    return jnp.concatenate([former * cosine - latter * sine_table, latter * cosine + former * sine_table], axis=-1)

def rotary_tables():
    half_dim = HEAD_DIM // 2
    freqs = jnp.power(10000.0, -jnp.arange(half_dim, dtype=jnp.float32) / half_dim)
    angles = jnp.arange(ROW, dtype=jnp.float32)[:, None] * freqs[None, :]
    return (jnp.cos(angles)[:, None, :], jnp.sin(angles)[:, None, :])

def attend(queries, key_rot, val_heads, segments):
    raw = low_back(jnp.einsum('qhd,khd->hqk', queries, key_rot, precision=HIGH))
    scores = raw * HEAD_DIM ** (-0.5)
    places = jnp.arange(ROW)
    allowed = (segments[:, None] == segments[None, :]) & (places[None, :] <= places[:, None])
    scores = jnp.where(allowed[None], scores, -1e+30)
    probs = low(jax.nn.softmax(scores, axis=-1))
    attended = jnp.einsum('hqk,khd->qhd', probs, val_heads, precision=HIGH)
    return both_ways(attended.reshape(ROW, HEADS * HEAD_DIM))

def layer(weights, row_input, segments, buckets):
    gain_one, bias_one, qkv_mat, proj_mat, gain_two, bias_two, up_mat, down_mat = weights
    attn_in = low(normalize(row_input, gain_one, bias_one))
    cosine, sine_table = rotary_tables()
    q_lin = low_back(jnp.dot(attn_in, qkv_mat[0], precision=HIGH))
    k_lin = low_back(jnp.dot(attn_in, qkv_mat[1], precision=HIGH))
    val_flat = both_ways(jnp.dot(attn_in, qkv_mat[2], precision=HIGH))
    queries = low(rotate(q_lin.reshape(ROW, HEADS, HEAD_DIM), cosine, sine_table))
    key_rot = low(rotate(k_lin.reshape(ROW, HEADS, HEAD_DIM), cosine, sine_table))
    attended = attend(queries, key_rot, val_flat.reshape(ROW, HEADS, HEAD_DIM), segments)
    mid_resid = row_input + low_back(jnp.dot(attended, proj_mat, precision=HIGH))
    ffn_in = low(normalize(mid_resid, gain_two, bias_two))
    hidden = low_back(jnp.dot(ffn_in, up_mat, precision=HIGH))
    limit = (buckets + 1) * (FF // 4)
    keep_mask = (jnp.arange(FF)[None, :] < limit[:, None]).astype(hidden.dtype)
    active = low(jnp.square(jnp.maximum(hidden, 0.0)) * keep_mask)
    return mid_resid + jnp.dot(active, down_mat, precision=HIGH)

def reference(inputs, segment_ids, width_bucket, attn_gain, attn_bias, qkv_weight, proj_weight, ffn_gain, ffn_bias, up_weight, down_weight, grad_result):
    weights = tuple((tensor_arg.astype(jnp.float32) for tensor_arg in (attn_gain, attn_bias, qkv_weight, proj_weight, ffn_gain, ffn_bias, up_weight, down_weight)))
    row_layer = jax.checkpoint(layer)

    def forward(all_inputs, *params):

        def advance(unused_state, row_items):
            return (unused_state, row_layer(params, row_items[0], row_items[1], row_items[2]))
        _, results = lax.scan(advance, None, (all_inputs.reshape(ROWS, ROW, D), segment_ids, width_bucket))
        return results.reshape(TOKENS, D)
    result, pullback = jax.vjp(forward, inputs.astype(jnp.float32), *weights)
    grads = pullback(grad_result.astype(jnp.float32))
    return (result.astype(jnp.bfloat16), grads[0], grads[1], grads[2], grads[3], grads[4], grads[5], grads[6], grads[7], grads[8])
```

```python
import functools

import jax
import jax.numpy as jnp
from jax import lax
from jax.experimental import pallas as pl
from jax.experimental.pallas import tpu as pltpu
from jax.sharding import PartitionSpec as P

HEAD_DIM = 128
FF = 8192
EPSILON = 1e-05
MASKED = -1e30
LONGEST_DOC = 512
QUERY_BLOCK = 256

bf16 = jnp.bfloat16
f32 = jnp.float32

NT = (((1,), (1,)), ((), ()))
TN = (((0,), (0,)), ((), ()))
NN = (((1,), (0,)), ((), ()))


def dot(a, b, dims):
    return lax.dot_general(a, b, dims, preferred_element_type=f32)


def block_probs(i, rot, seg_row, seg_col, block, scale):
    start = i * block
    low = max(0, start - LONGEST_DOC)
    high = start + block
    q = rot[0, start:high, :]
    k = rot[1, low:high, :]
    scores = dot(q, k, NT) * scale
    shape = scores.shape
    q_pos = start + lax.broadcasted_iota(jnp.int32, shape, 0)
    k_pos = low + lax.broadcasted_iota(jnp.int32, shape, 1)
    allowed = (seg_col[start:high, :] == seg_row[0][:, low:high]) & (k_pos <= q_pos)
    scores = jnp.where(allowed, scores, MASKED)
    expo = jnp.exp(scores - jnp.max(scores, axis=1, keepdims=True))
    return expo * (1.0 / jnp.sum(expo, axis=1, keepdims=True)), q, k, start, low, high


def attn_fwd_kernel(block, scale, q_lin, k_lin, v_lin, cosine, sine, seg_row, seg_col, att, rot):
    cos_t = cosine[...]
    sin_t = sine[...]
    for s, lin in ((0, q_lin), (1, k_lin)):
        z = lin[...]
        rot[s] = (z * cos_t + pltpu.roll(z, HEAD_DIM // 2, 1) * sin_t).astype(bf16)
    rot[2] = v_lin[...].astype(bf16)
    for i in range(q_lin.shape[0] // block):
        probs, _, _, start, low, high = block_probs(i, rot, seg_row, seg_col, block, scale)
        att[start:high, :] = dot(probs.astype(bf16), rot[2, low:high, :], NN).astype(bf16)


def attn_bwd_kernel(block, scale, rot, g_att, cosine, sine, seg_row, seg_col, grads, dk, dv):
    cos_t = cosine[...]
    sin_t = sine[...]
    cols = grads.shape[1] // 3
    at = pl.program_id(1) * HEAD_DIM
    dk[...] = jnp.zeros_like(dk)
    dv[...] = jnp.zeros_like(dv)

    def lanes(s):
        return pl.ds(pl.multiple_of(s * cols + at, HEAD_DIM), HEAD_DIM)

    def back(z, c, s):
        return (z * c - pltpu.roll(z, HEAD_DIM // 2, 1) * s).astype(bf16)

    for i in range(rot.shape[1] // block):
        probs, q, k, start, low, high = block_probs(i, rot, seg_row, seg_col, block, scale)
        g = g_att[start:high, :]
        g_probs = dot(g, rot[2, low:high, :], NT)
        delta = jnp.sum(probs * g_probs, axis=1, keepdims=True)
        g_raw = (probs * (g_probs - delta) * scale).astype(bf16)
        grads[start:high, lanes(0)] = back(
            dot(g_raw, k, NN), cos_t[start:high, :], sin_t[start:high, :]
        )
        dk[low:high, :] += dot(g_raw, q, TN)
        dv[low:high, :] += dot(probs.astype(bf16), g, TN)
    grads[:, lanes(1)] = back(dk[...], cos_t, sin_t)
    grads[:, lanes(2)] = dv[...].astype(bf16)


def attention_specs(row_len):
    triple = pl.BlockSpec((3, row_len, HEAD_DIM), lambda r, h: (0, r, h))
    plain = pl.BlockSpec((row_len, HEAD_DIM), lambda r, h: (r, h))
    table = pl.BlockSpec((row_len, HEAD_DIM), lambda r, h: (0, 0))
    seg_row = pl.BlockSpec((1, 1, row_len), lambda r, h: (r, 0, 0))
    seg_col = pl.BlockSpec((row_len, 1), lambda r, h: (r, 0))
    return triple, plain, table, seg_row, seg_col


def attn_forward(lin, cos_t, sin_t, segs):
    tokens = lin.shape[0]
    cols = lin.shape[1] // 3
    heads = cols // HEAD_DIM
    rows, row_len = segs.shape
    triple, plain, table, seg_row, seg_col = attention_specs(row_len)
    block = min(QUERY_BLOCK, row_len)
    parts = [
        pl.BlockSpec((row_len, HEAD_DIM), lambda r, h, s=s: (r, s * heads + h)) for s in range(3)
    ]
    return pl.pallas_call(
        functools.partial(attn_fwd_kernel, block, HEAD_DIM**-0.5),
        grid=(rows, heads),
        in_specs=[*parts, table, table, seg_row, seg_col],
        out_specs=[plain, triple],
        out_shape=[
            jax.ShapeDtypeStruct((tokens, cols), bf16),
            jax.ShapeDtypeStruct((3, tokens, cols), bf16),
        ],
        compiler_params=pltpu.CompilerParams(vmem_limit_bytes=32 * 2**20),
    )(lin, lin, lin, cos_t, sin_t, segs[:, None, :], segs.reshape(tokens, 1))


def attn_backward(rot, g_att, cos_t, sin_t, segs):
    _, tokens, cols = rot.shape
    rows, row_len = segs.shape
    triple, plain, table, seg_row, seg_col = attention_specs(row_len)
    block = min(QUERY_BLOCK, row_len)
    return pl.pallas_call(
        functools.partial(attn_bwd_kernel, block, HEAD_DIM**-0.5),
        grid=(rows, cols // HEAD_DIM),
        in_specs=[triple, plain, table, table, seg_row, seg_col],
        out_specs=pl.BlockSpec((row_len, 3 * cols), lambda r, h: (r, 0)),
        out_shape=jax.ShapeDtypeStruct((tokens, 3 * cols), bf16),
        scratch_shapes=[pltpu.VMEM((row_len, HEAD_DIM), f32)] * 2,
        compiler_params=pltpu.CompilerParams(vmem_limit_bytes=32 * 2**20),
    )(rot, g_att, cos_t, sin_t, segs[:, None, :], segs.reshape(tokens, 1))


def after(value, *deps):
    return lax.optimization_barrier((value,) + deps)[0]


def join_kernel(n, chunks, *refs):
    per = 2 * n - 1
    out, sem = refs[chunks * per], refs[chunks * per + 1]
    me = lax.axis_index("mp")
    at = 0
    for c in range(chunks):
        own, right, left = refs[c * per], refs[c * per + 1 : c * per + n], refs[c * per + n : c * per + per]
        rows, cols = own.shape

        def put(src, block, at=at, rows=rows, cols=cols):
            target = out.at[
                pl.ds(at, rows), pl.ds(pl.multiple_of(block * cols, cols), cols)
            ]
            pltpu.make_async_copy(src, target, sem).start()

        at += rows
        put(own, me)
        for s in range(1, n):
            pl.when(me >= s)(functools.partial(put, right[s - 1], me - s))
            pl.when(me + s < n)(functools.partial(put, left[s - 1], me + s))
    pltpu.make_async_copy(out, out, sem).wait()


def join(parts):
    n = lax.axis_size("mp")
    rows = sum(p[0].shape[0] for p in parts)
    flat = [a for own, right, left in parts for a in (own, *right, *left)]
    shape = (rows, n * parts[0][0].shape[1])
    return pl.pallas_call(
        functools.partial(join_kernel, n, len(parts)),
        in_specs=[pl.BlockSpec(memory_space=pl.ANY)] * len(flat),
        out_specs=pl.BlockSpec(memory_space=pltpu.VMEM),
        out_shape=jax.ShapeDtypeStruct(shape, parts[0][0].dtype),
        scratch_shapes=[pltpu.SemaphoreType.DMA(())],
        compiler_params=pltpu.CompilerParams(vmem_limit_bytes=32 * 2**20),
    )(*flat)


def line_step(s, right, left):
    n = lax.axis_size("mp")
    return (
        lax.ppermute(right, "mp", [(i, i + 1) for i in range(s - 1, n - 1)]),
        lax.ppermute(left, "mp", [(i, i - 1) for i in range(1, n - s + 1)]),
    )


def line_parts(block, first=None):
    right = left = block
    rights, lefts = [], []
    for s in range(1, lax.axis_size("mp")):
        if s == 1 and first is not None:
            right, left = first
        else:
            right, left = line_step(s, right, left)
        rights.append(right)
        lefts.append(left)
    return block, rights, lefts


def line_gather(chunks):
    return join([line_parts(c) for c in chunks])


def split_rows(x, chunks=2):
    return jnp.split(x, chunks, axis=0)


def line_scatter(chunks, beside=()):
    n = lax.axis_size("mp")
    me = lax.axis_index("mp")
    cols = chunks[0].shape[1] // n

    def block(y, j):
        return lax.dynamic_slice_in_dim(y, jnp.clip(j, 0, n - 1) * cols, cols, 1)

    def add(*terms):
        return sum(t.astype(f32) for t in terms)

    pairs = [(block(y, me + n - 1), block(y, me - n + 1)) for y in chunks]
    for s in range(1, n):
        pairs = [
            (
                lax.ppermute(right, "mp", [(i, i + 1) for i in range(s)]),
                lax.ppermute(left, "mp", [(i, i - 1) for i in range(n - s, n)]),
            )
            for right, left in pairs
        ]
        if s < n - 1:
            pairs = [
                (
                    add(right, block(y, me + n - s - 1)).astype(bf16),
                    add(left, block(y, me - n + s + 1)).astype(bf16),
                )
                for (right, left), y in zip(pairs, chunks)
            ]
            if s <= len(beside):
                pairs = [tuple(after(a, beside[s - 1]) for a in pair) for pair in pairs]
    sums = [add(right, left, block(y, me)) for (right, left), y in zip(pairs, chunks)]
    return jnp.concatenate(sums) if len(sums) > 1 else sums[0]


class Halving:
    def __init__(self, make):
        size = lax.axis_size("dp")
        me = lax.axis_index("dp")
        odd = me & 1
        self.odd = odd
        rest = list(range(1, size.bit_length() - 1))
        steps = []
        for even_bit, odd_bit in zip(rest, rest[1:] + rest[:1]):
            bit = jnp.where(odd == 1, (me >> odd_bit) & 1, (me >> even_bit) & 1)
            steps.append(((even_bit, odd_bit), bit))
        self.todo = [(True, *s) for s in steps] + [(False, *s) for s in reversed(steps)]
        sent = make(1 - odd)
        self.x = kept = make(after(odd, sent))
        self.flight = (True, odd, kept, self.exchange(sent, (0, 0)))
        self.last = None

    def exchange(self, x, bits):
        size = lax.axis_size("dp")
        return lax.ppermute(x, "dp", [(i, i ^ (1 << bits[i & 1])) for i in range(size)])

    def launch(self):
        if self.flight is not None or self.last is not None:
            return
        if not self.todo:
            self.last = self.exchange(self.x, (0, 0))
            return
        halve, bits, bit = self.todo.pop(0)
        kept = sent = self.x
        if halve:
            half = self.x.shape[0] // 2
            kept = lax.dynamic_slice_in_dim(self.x, bit * half, half, 0)
            sent = lax.dynamic_slice_in_dim(self.x, (1 - bit) * half, half, 0)
        self.flight = (halve, bit, kept, self.exchange(sent, bits))

    def land(self):
        if self.flight is None:
            return
        halve, bit, kept, got = self.flight
        if halve:
            self.x = (kept.astype(f32) + got.astype(f32)).astype(bf16)
        else:
            self.x = jnp.where(
                bit == 0, jnp.concatenate([kept, got]), jnp.concatenate([got, kept])
            )
        self.flight = None

    def finish(self, groups=1):
        while self.last is None:
            self.land()
            self.launch()
        return widen(self.x, self.last, self.odd, groups)


def widen_kernel(odd, own, other, out):
    groups, _, cols = out.shape

    def put(src):
        for g in range(groups):
            out[g] = src[:, g * cols : (g + 1) * cols].astype(f32)

    pl.when(pl.program_id(0) == 0)(functools.partial(put, own))
    pl.when(pl.program_id(0) == 1)(functools.partial(put, other))


def widen(own, other, odd, groups):
    rows, cols = own.shape
    block = min(256, rows)
    count = rows // block
    wide = cols // groups
    return pl.pallas_call(
        widen_kernel,
        grid_spec=pltpu.PrefetchScalarGridSpec(
            num_scalar_prefetch=1,
            grid=(2, count),
            in_specs=[
                pl.BlockSpec((block, cols), lambda k, r, odd: (jnp.where(k == 0, r, count - 1), 0)),
                pl.BlockSpec((block, cols), lambda k, r, odd: (jnp.where(k == 1, r, 0), 0)),
            ],
            out_specs=pl.BlockSpec(
                (groups, block, wide),
                lambda k, r, odd: (0, jnp.where(k == 0, odd[0], 1 - odd[0]) * count + r, 0),
            ),
        ),
        out_shape=jax.ShapeDtypeStruct((groups, 2 * rows, wide), f32),
        compiler_params=pltpu.CompilerParams(vmem_limit_bytes=32 * 2**20),
    )(odd.reshape(1).astype(jnp.int32), own, other)


def half_lanes(x, half):
    size = x.shape[1] // 2
    return lax.dynamic_slice_in_dim(x, half * size, size, 1)


def meet(values, *sums):
    for h in sums:
        h.land()
    met = lax.optimization_barrier((*values, *(h.x for h in sums)))
    for h, x in zip(sums, met[len(values) :]):
        h.x = x
        h.launch()
    return met[: len(values)]


def butterfly_sum(x, axis):
    size = lax.axis_size(axis)
    for bit in range(size.bit_length() - 1):
        x = x + lax.ppermute(x, axis, [(i, i ^ (1 << bit)) for i in range(size)])
    return x


def split_bits(v):
    high = lax.reduce_precision(v, 8, 7)
    return [high.astype(bf16), (v - high).astype(bf16)]


def normalize(v):
    mean = jnp.mean(v, axis=1, keepdims=True)
    centred = v - mean
    rstd = lax.rsqrt(jnp.mean(centred * centred, axis=1, keepdims=True) + EPSILON)
    return centred * rstd, rstd


def local(
    inputs,
    segment_ids,
    width_bucket,
    attn_gain,
    attn_bias,
    qkv_weight,
    proj_weight,
    ffn_gain,
    ffn_bias,
    up_weight,
    down_weight,
    grad_result,
):
    tokens, feats = inputs.shape
    row_len = segment_ids.shape[1]
    mp_size = lax.axis_size("mp")
    dp_size = lax.axis_size("dp")
    mp_idx = lax.axis_index("mp")
    width = feats * mp_size

    def own(a):
        return lax.dynamic_slice_in_dim(a, mp_idx * feats, feats, a.ndim - 1)

    half = HEAD_DIM // 2
    freqs = jnp.power(10000.0, -jnp.arange(half, dtype=f32) / half)
    angles = jnp.arange(row_len, dtype=f32)[:, None] * freqs[None, :]
    cos_h, sin_h = jnp.cos(angles), jnp.sin(angles)
    cos_t = jnp.concatenate([cos_h, cos_h], axis=1)
    sin_t = jnp.concatenate([-sin_h, sin_h], axis=1)

    vectors = sum((split_bits(v) for v in (attn_gain, attn_bias, ffn_gain, ffn_bias)), [])
    packed = jnp.concatenate([jnp.stack(vectors), jnp.zeros((8, feats), bf16)])
    first, second = split_rows(inputs)
    chunks = [first, jnp.concatenate([second, packed])]
    starts = [line_step(1, c, c) for c in chunks]
    gathered = join([line_parts(c, pair) for c, pair in zip(chunks, starts)])
    vec = gathered[tokens : tokens + 8].astype(f32)
    gain_a, bias_a, gain_f, bias_f = (vec[2 * i] + vec[2 * i + 1] for i in range(4))
    x = gathered[:tokens].astype(f32)
    gy_first, gy_second = split_rows(grad_result)
    gy_first = lax.all_gather(after(gy_first, gathered), "mp", axis=1, tiled=True)

    part = width // dp_size
    slab = lax.dynamic_slice_in_dim(proj_weight, lax.axis_index("dp") * part, part, 1)
    slab = lax.all_gather(slab, "mp", axis=0, tiled=True)
    proj_full = lax.all_gather(after(slab, starts[0][0]), "dp", axis=1, tiled=True)

    qkv_all = jnp.concatenate([qkv_weight[s] for s in range(3)], axis=1)
    xhat_a, rstd_a = normalize(x)
    attn_rows = (xhat_a * gain_a + bias_a).astype(bf16)
    att, rot = attn_forward(dot(attn_rows, qkv_all, NN), cos_t, sin_t, segment_ids)
    att_full, gy_first = lax.optimization_barrier((line_gather(split_rows(att)), gy_first))
    gy_second = lax.all_gather(after(gy_second, att_full), "mp", axis=1, tiled=True)

    mid = x + dot(att_full, after(proj_full, att_full), NN)
    xhat_f, rstd_f = normalize(mid)
    ffn_rows = (xhat_f * gain_f + bias_f).astype(bf16)

    limit = (width_bucket.reshape(tokens) + 1) * (FF // 4)
    columns = mp_idx * up_weight.shape[1] + jnp.arange(up_weight.shape[1], dtype=jnp.int32)
    keep = columns[None, :] < limit[:, None]
    hidden = dot(ffn_rows, up_weight, NN)
    relu = jnp.where(keep, jnp.maximum(hidden, 0.0), 0.0)
    active = (relu * relu).astype(bf16)

    gy_first = after(gy_first, active)
    halves = []
    for g, r in zip((gy_first, gy_second), split_rows(relu)):
        halves.append((2.0 * r * dot(g, down_weight, NT)).astype(bf16))
        gy_second = after(gy_second, halves[0])
    grad_hidden = jnp.concatenate(halves)
    g_ffn_part = dot(grad_hidden, up_weight, NT).astype(bf16)
    g_ffn_own = lax.psum_scatter(g_ffn_part, "mp", scatter_dimension=1, tiled=True)

    active, gy_first, gy_second = (after(a, g_ffn_part) for a in (active, gy_first, gy_second))
    gy = jnp.concatenate([gy_first, gy_second])
    down = Halving(lambda half: dot(half_lanes(active, half), gy, TN).astype(bf16))
    grad_up = dot(after(ffn_rows, down.x), grad_hidden, TN).astype(bf16)
    (grad_up,) = meet((grad_up,), down)
    grad_up = lax.psum(grad_up, "dp")
    ffn_part = dot(after(active, down.x), down_weight, NN).astype(bf16)
    g_ffn_own, ffn_part = lax.optimization_barrier((g_ffn_own, ffn_part))
    chunks = split_rows(g_ffn_own)
    (chunks[0],) = meet((chunks[0],), down)
    parts = [(c, [], []) for c in chunks]
    ends = [(c, c) for c in chunks]
    for s in range(1, mp_size):
        ends = [line_step(s, *pair) for pair in ends]
        if s < mp_size - 1:
            ends[0] = meet(ends[0], down)
        for (_, rights, lefts), (right, left) in zip(parts, ends):
            rights.append(right)
            lefts.append(left)
    (g_ffn,) = meet((join(parts),), down)
    ffn_part = after(ffn_part, g_ffn)
    ffn_out = lax.psum_scatter(ffn_part, "mp", scatter_dimension=1, tiled=True)
    g_ffn = g_ffn.astype(f32)

    scaled = g_ffn * gain_f
    grad_mid = gy.astype(f32) + rstd_f * (
        scaled
        - jnp.mean(scaled, axis=1, keepdims=True)
        - xhat_f * jnp.mean(scaled * xhat_f, axis=1, keepdims=True)
    )
    grad_mid_low = grad_mid.astype(bf16)
    g_att = dot(grad_mid_low, proj_weight, NT).astype(bf16)
    (g_att,) = meet((g_att,), down)
    g_qkv_rows = attn_backward(rot, g_att, cos_t, sin_t, segment_ids)
    qkv = Halving(lambda half: dot(half_lanes(attn_rows, half), g_qkv_rows, TN).astype(bf16))
    later = after(g_qkv_rows, qkv.x)
    g_attn_part = dot(later, qkv_all, NT)
    g_attn_low = g_attn_part.astype(bf16)
    (g_attn_low,) = meet((g_attn_low,), qkv)
    g_attn = lax.psum_scatter(g_attn_low, "mp", scatter_dimension=1, tiled=True).astype(f32)
    mid_later = after(grad_mid_low, g_attn_low)
    proj = Halving(lambda half: dot(half_lanes(att, half), mid_later, TN).astype(bf16))
    grad_down = down.finish()[0]
    grad_qkv, grad_proj = qkv.finish(3), proj.finish()[0]

    part_scaled = g_attn_part * gain_a
    sums = butterfly_sum(
        jnp.stack([jnp.sum(part_scaled, axis=1), jnp.sum(part_scaled * xhat_a, axis=1)]), "mp"
    )
    sum_plain, sum_cross = sums[0][:, None], sums[1][:, None]
    g_ffn_mine = g_ffn_own.astype(f32)
    ffn_vec = jnp.stack(
        [jnp.sum(g_ffn_mine * own(xhat_f), axis=0), jnp.sum(g_ffn_mine, axis=0)]
    )
    attn_vec = jnp.stack([jnp.sum(g_attn_part * xhat_a, axis=0), jnp.sum(g_attn_part, axis=0)])
    attn_vec = own(butterfly_sum(attn_vec, "mp"))
    grad_vec = butterfly_sum(jnp.concatenate([attn_vec, ffn_vec]), "dp")
    grad_input = own(grad_mid) + rstd_a * (
        g_attn * attn_gain - sum_plain / width - own(xhat_a) * (sum_cross / width)
    )
    block_output = (own(mid) + ffn_out.astype(f32)).astype(bf16)
    return (
        block_output,
        grad_input,
        grad_vec[0],
        grad_vec[1],
        grad_qkv,
        grad_proj,
        grad_vec[2],
        grad_vec[3],
        grad_up.astype(f32),
        grad_down,
    )


def solution(mesh):
    placed = (
        P("dp", "mp"),
        P("dp", None),
        P("dp", None),
        P("mp"),
        P("mp"),
        P(None, None, "mp"),
        P("mp", None),
        P("mp"),
        P("mp"),
        P(None, "mp"),
        P("mp", None),
        P("dp", "mp"),
    )
    return jax.shard_map(
        local,
        mesh=mesh,
        in_specs=placed,
        out_specs=(
            P("dp", "mp"),
            P("dp", "mp"),
            P("mp"),
            P("mp"),
            P(None, None, "mp"),
            P("mp", None),
            P("mp"),
            P("mp"),
            P(None, "mp"),
            P("mp", None),
        ),
        check_vma=False,
    )
```

```python
import functools

import jax
import jax.numpy as jnp
from jax import lax
from jax.experimental import pallas as pl
from jax.experimental.pallas import tpu as pltpu
from jax.sharding import PartitionSpec as P

HEAD_DIM = 128
FF = 8192
EPSILON = 1e-05
MASKED = -1e30
LONGEST_DOC = 512
QUERY_BLOCK = 256
VMEM = 36 * 2**20
COST = pl.CostEstimate(flops=1, bytes_accessed=1, transcendentals=0)

bf16 = jnp.bfloat16
f32 = jnp.float32

NT = (((1,), (1,)), ((), ()))
TN = (((0,), (0,)), ((), ()))
NN = (((1,), (0,)), ((), ()))


def dot(a, b, dims):
    return lax.dot_general(a, b, dims, preferred_element_type=f32)


def block_probs(i, rot, seg_row, seg_col, block, scale):
    start = i * block
    low = max(0, start - LONGEST_DOC)
    high = start + block
    q = rot[0, start:high, :]
    k = rot[1, low:high, :]
    scores = dot(q, k, NT) * scale
    shape = scores.shape
    q_pos = start + lax.broadcasted_iota(jnp.int32, shape, 0)
    k_pos = low + lax.broadcasted_iota(jnp.int32, shape, 1)
    allowed = (seg_col[start:high, :] == seg_row[0][:, low:high]) & (k_pos <= q_pos)
    scores = jnp.where(allowed, scores, MASKED)
    expo = jnp.exp(scores - jnp.max(scores, axis=1, keepdims=True))
    return expo * (1.0 / jnp.sum(expo, axis=1, keepdims=True)), q, k, start, low, high


def attn_fwd_kernel(block, scale, q_lin, k_lin, v_lin, cosine, sine, seg_row, seg_col, att, rot):
    cos_t = cosine[...]
    sin_t = sine[...]
    for s, lin in ((0, q_lin), (1, k_lin)):
        z = lin[...]
        rot[s] = (z * cos_t + pltpu.roll(z, HEAD_DIM // 2, 1) * sin_t).astype(bf16)
    rot[2] = v_lin[...].astype(bf16)
    for i in range(q_lin.shape[0] // block):
        probs, _, _, start, low, high = block_probs(i, rot, seg_row, seg_col, block, scale)
        att[start:high, :] = dot(probs.astype(bf16), rot[2, low:high, :], NN).astype(bf16)


def attn_bwd_kernel(block, scale, rot, g_att, cosine, sine, seg_row, seg_col, grads, dk, dv):
    cos_t = cosine[...]
    sin_t = sine[...]
    cols = grads.shape[1] // 3
    at = pl.program_id(1) * HEAD_DIM
    dk[...] = jnp.zeros_like(dk)
    dv[...] = jnp.zeros_like(dv)

    def lanes(s):
        return pl.ds(pl.multiple_of(s * cols + at, HEAD_DIM), HEAD_DIM)

    def back(z, c, s):
        return (z * c - pltpu.roll(z, HEAD_DIM // 2, 1) * s).astype(bf16)

    for i in range(rot.shape[1] // block):
        probs, q, k, start, low, high = block_probs(i, rot, seg_row, seg_col, block, scale)
        g = g_att[start:high, :]
        g_probs = dot(g, rot[2, low:high, :], NT)
        delta = jnp.sum(probs * g_probs, axis=1, keepdims=True)
        g_raw = (probs * (g_probs - delta) * scale).astype(bf16)
        grads[start:high, lanes(0)] = back(
            dot(g_raw, k, NN), cos_t[start:high, :], sin_t[start:high, :]
        )
        dk[low:high, :] += dot(g_raw, q, TN)
        dv[low:high, :] += dot(probs.astype(bf16), g, TN)
    grads[:, lanes(1)] = back(dk[...], cos_t, sin_t)
    grads[:, lanes(2)] = dv[...].astype(bf16)


def attention_specs(row_len):
    triple = pl.BlockSpec((3, row_len, HEAD_DIM), lambda r, h: (0, r, h))
    plain = pl.BlockSpec((row_len, HEAD_DIM), lambda r, h: (r, h))
    table = pl.BlockSpec((row_len, HEAD_DIM), lambda r, h: (0, 0))
    seg_row = pl.BlockSpec((1, 1, row_len), lambda r, h: (r, 0, 0))
    seg_col = pl.BlockSpec((row_len, 1), lambda r, h: (r, 0))
    return triple, plain, table, seg_row, seg_col


def attn_forward(lin, cos_t, sin_t, segs):
    tokens = lin.shape[0]
    cols = lin.shape[1] // 3
    heads = cols // HEAD_DIM
    rows, row_len = segs.shape
    triple, plain, table, seg_row, seg_col = attention_specs(row_len)
    block = min(QUERY_BLOCK, row_len)
    parts = [
        pl.BlockSpec((row_len, HEAD_DIM), lambda r, h, s=s: (r, s * heads + h)) for s in range(3)
    ]
    return pl.pallas_call(
        functools.partial(attn_fwd_kernel, block, HEAD_DIM**-0.5),
        grid=(rows, heads),
        in_specs=[*parts, table, table, seg_row, seg_col],
        out_specs=[plain, triple],
        out_shape=[
            jax.ShapeDtypeStruct((tokens, cols), bf16),
            jax.ShapeDtypeStruct((3, tokens, cols), bf16),
        ],
        compiler_params=pltpu.CompilerParams(vmem_limit_bytes=VMEM),
        cost_estimate=COST,
    )(lin, lin, lin, cos_t, sin_t, segs[:, None, :], segs.reshape(tokens, 1))


def attn_backward(rot, g_att, cos_t, sin_t, segs):
    _, tokens, cols = rot.shape
    rows, row_len = segs.shape
    triple, plain, table, seg_row, seg_col = attention_specs(row_len)
    block = min(QUERY_BLOCK, row_len)
    return pl.pallas_call(
        functools.partial(attn_bwd_kernel, block, HEAD_DIM**-0.5),
        grid=(rows, cols // HEAD_DIM),
        in_specs=[triple, plain, table, table, seg_row, seg_col],
        out_specs=pl.BlockSpec((row_len, 3 * cols), lambda r, h: (r, 0)),
        out_shape=jax.ShapeDtypeStruct((tokens, 3 * cols), bf16),
        scratch_shapes=[pltpu.VMEM((row_len, HEAD_DIM), f32)] * 2,
        compiler_params=pltpu.CompilerParams(vmem_limit_bytes=VMEM),
        cost_estimate=COST,
    )(rot, g_att, cos_t, sin_t, segs[:, None, :], segs.reshape(tokens, 1))


def after(value, *deps):
    return lax.optimization_barrier((value,) + deps)[0]


def join_kernel(n, chunks, *refs):
    per = 2 * n - 1
    out, sem = refs[chunks * per], refs[chunks * per + 1]
    me = lax.axis_index("mp")
    at = 0
    for c in range(chunks):
        own, right, left = refs[c * per], refs[c * per + 1 : c * per + n], refs[c * per + n : c * per + per]
        rows, cols = own.shape

        def put(src, block, at=at, rows=rows, cols=cols):
            target = out.at[
                pl.ds(at, rows), pl.ds(pl.multiple_of(block * cols, cols), cols)
            ]
            pltpu.make_async_copy(src, target, sem).start()

        at += rows
        put(own, me)
        for s in range(1, n):
            pl.when(me >= s)(functools.partial(put, right[s - 1], me - s))
            pl.when(me + s < n)(functools.partial(put, left[s - 1], me + s))
    pltpu.make_async_copy(out, out, sem).wait()


def join(parts):
    n = lax.axis_size("mp")
    rows = sum(p[0].shape[0] for p in parts)
    flat = [a for own, right, left in parts for a in (own, *right, *left)]
    shape = (rows, n * parts[0][0].shape[1])
    return pl.pallas_call(
        functools.partial(join_kernel, n, len(parts)),
        in_specs=[pl.BlockSpec(memory_space=pl.ANY)] * len(flat),
        out_specs=pl.BlockSpec(memory_space=pltpu.VMEM),
        out_shape=jax.ShapeDtypeStruct(shape, parts[0][0].dtype),
        scratch_shapes=[pltpu.SemaphoreType.DMA(())],
        compiler_params=pltpu.CompilerParams(vmem_limit_bytes=VMEM),
        cost_estimate=COST,
    )(*flat)


def line_step(s, right, left):
    n = lax.axis_size("mp")
    return (
        lax.ppermute(right, "mp", [(i, i + 1) for i in range(s - 1, n - 1)]),
        lax.ppermute(left, "mp", [(i, i - 1) for i in range(1, n - s + 1)]),
    )


def line_parts(block, first=None):
    right = left = block
    rights, lefts = [], []
    for s in range(1, lax.axis_size("mp")):
        if s == 1 and first is not None:
            right, left = first
        else:
            right, left = line_step(s, right, left)
        rights.append(right)
        lefts.append(left)
    return block, rights, lefts


def line_gather(chunks):
    return join([line_parts(c) for c in chunks])


def split_rows(x, chunks=2):
    return jnp.split(x, chunks, axis=0)


class Scatter:
    def __init__(self, y):
        self.n = lax.axis_size("mp")
        self.me = lax.axis_index("mp")
        self.y = y
        self.step = 0
        self.x = (self.block(self.n - 1), self.block(1 - self.n))
        self.flight = None
        self.launch()

    def block(self, offset):
        cols = self.y.shape[1] // self.n
        at = jnp.clip(self.me + offset, 0, self.n - 1) * cols
        return lax.dynamic_slice_in_dim(self.y, at, cols, 1)

    def launch(self):
        self.step += 1
        n, s = self.n, self.step
        if s < n:
            right, left = self.x
            self.flight = (
                lax.ppermute(right, "mp", [(i, i + 1) for i in range(s)]),
                lax.ppermute(left, "mp", [(i, i - 1) for i in range(n - s, n)]),
            )

    def land(self):
        if self.flight is not None:
            ahead = self.n - self.step - 1
            self.x = self.flight
            if ahead > 0:
                self.x = tuple(
                    (a.astype(f32) + self.block(offset).astype(f32)).astype(bf16)
                    for a, offset in zip(self.x, (ahead, -ahead))
                )
            self.flight = None

    def finish(self):
        while self.flight is not None:
            self.land()
            self.launch()
        return sum(a.astype(f32) for a in (*self.x, self.block(0)))


def dp_pairs(bits):
    return [(i, i ^ (1 << bits[i & 1])) for i in range(lax.axis_size("dp"))]


def dp_rounds():
    rest = list(range(1, lax.axis_size("dp").bit_length() - 1))
    return list(zip(rest, rest[1:] + rest[:1]))


def by_parity(odd, bits, value):
    return jnp.where(odd == 1, value(bits[1]), value(bits[0]))


class Pieces:
    def __init__(self, piece, place, rounds):
        self.x = (piece,)
        self.flight = None
        self.me = lax.axis_index("dp")
        self.owners = [self.me]
        self.place = place
        self.rounds = list(reversed(rounds))
        self.todo = self.rounds + [(0, 0)]

    def launch(self):
        if self.todo and self.flight is None:
            bits = self.todo.pop(0)
            if self.todo and len(self.x) > 1:
                self.x = (jnp.concatenate(self.x),)
            got = tuple(lax.ppermute(p, "dp", dp_pairs(bits)) for p in self.x)
            self.flight = (bits, got)

    def land(self):
        if self.flight is None:
            return
        bits, got = self.flight
        self.flight = None
        self.x = self.x + got
        if self.todo:
            flip = by_parity(self.me & 1, bits, lambda b: 1 << b)
            self.owners = self.owners + [o ^ flip for o in self.owners]
        else:
            theirs = [self.me ^ 1]
            for bits in self.rounds:
                flip = by_parity(1 - (self.me & 1), bits, lambda b: 1 << b)
                theirs = theirs + [o ^ flip for o in theirs]
            self.owners = self.owners + theirs

    def finish(self, groups=1):
        while self.todo or self.flight is not None:
            self.land()
            self.launch()
        return widen(self.x, jnp.stack([self.place(o) for o in self.owners]), groups)


class Halving:
    def __init__(self, make, whole=False):
        self.me = lax.axis_index("dp")
        odd = self.me & 1
        self.todo = dp_rounds()
        self.whole = whole
        self.pieces = None
        sent = make(1 - odd)
        self.x = (make(after(odd, sent)),)
        self.flight = lax.ppermute(sent, "dp", dp_pairs((0, 0)))

    def place(self, device):
        odd = device & 1
        at = odd
        if not self.whole:
            for bits in dp_rounds():
                at = at * 2 + by_parity(odd, bits, lambda b: (device >> b) & 1)
        return at

    def launch(self):
        if self.pieces is not None:
            self.pieces.x = self.x
            self.pieces.launch()
        elif self.todo and self.flight is None:
            bits = self.todo.pop(0)
            *kept, sent = self.x
            self.x = tuple(kept) or (sent,)
            self.flight = lax.ppermute(sent, "dp", dp_pairs(bits))

    def land(self):
        if self.pieces is not None:
            self.pieces.land()
            self.x = self.pieces.x
        elif self.flight is not None:
            (kept,) = self.x
            got = self.flight
            self.flight = None

            def add(at=0, rows=kept.shape[0]):
                terms = (lax.dynamic_slice_in_dim(a, at, rows, 0) for a in (kept, got))
                return sum(a.astype(f32) for a in terms).astype(bf16)

            if not self.todo:
                self.x = (add(),)
                rounds = [] if self.whole else dp_rounds()
                self.pieces = Pieces(self.x[0], self.place, rounds)
            elif self.whole:
                self.x = (add(),)
            else:
                half = kept.shape[0] // 2
                bit = by_parity(self.me & 1, self.todo[0], lambda b: (self.me >> b) & 1)
                self.x = (add(bit * half, half), add((1 - bit) * half, half))

    def finish(self, groups=1):
        while self.pieces is None:
            self.land()
            self.launch()
        self.pieces.x = self.x
        return self.pieces.finish(groups)


def widen_kernel(firsts, table, *refs):
    *arrays, out = refs
    groups, _, cols = out.shape
    step = pl.program_id(0)
    for k, src in enumerate(arrays):

        @pl.when((step >= firsts[k]) & (step < firsts[k + 1]))
        def _(src=src):
            for g in range(groups):
                out[g] = src[:, g * cols : (g + 1) * cols].astype(f32)


def widen(arrays, places, groups):
    total = sum(a.shape[0] for a in arrays)
    cols = arrays[0].shape[1]
    rows = total // places.shape[0]
    block = min(256, rows)
    per = rows // block
    wide = cols // groups
    firsts = [sum(a.shape[0] for a in arrays[:k]) // block for k in range(len(arrays) + 1)]

    def spec(k):
        def index(step, table):
            return (jnp.clip(step - firsts[k], 0, firsts[k + 1] - firsts[k] - 1), 0)

        return pl.BlockSpec((block, cols), index)

    def out_index(step, table):
        return (0, table[step // per] * per + step % per, 0)

    return pl.pallas_call(
        functools.partial(widen_kernel, firsts),
        grid_spec=pltpu.PrefetchScalarGridSpec(
            num_scalar_prefetch=1,
            grid=(total // block,),
            in_specs=[spec(k) for k in range(len(arrays))],
            out_specs=pl.BlockSpec((groups, block, wide), out_index),
        ),
        out_shape=jax.ShapeDtypeStruct((groups, total, wide), f32),
        compiler_params=pltpu.CompilerParams(vmem_limit_bytes=VMEM),
        cost_estimate=COST,
    )(places.astype(jnp.int32), *arrays)


def half_lanes(x, half):
    size = x.shape[1] // 2
    return lax.dynamic_slice_in_dim(x, half * size, size, 1)


def meet(values, *sums):
    for h in sums:
        h.land()
    met, xs = lax.optimization_barrier((tuple(values), tuple(h.x for h in sums)))
    for h, x in zip(sums, xs):
        h.x = x
        h.launch()
    return met


def butterfly_sum(x, axis):
    size = lax.axis_size(axis)
    for bit in range(size.bit_length() - 1):
        x = x + lax.ppermute(x, axis, [(i, i ^ (1 << bit)) for i in range(size)])
    return x


def norm_qkv_kernel(x, weight, gain, bias, rows, lin):
    v = x[...].astype(f32)
    centred = v - jnp.mean(v, axis=1, keepdims=True)
    rstd = lax.rsqrt(jnp.mean(centred * centred, axis=1, keepdims=True) + EPSILON)
    normed = (centred * rstd * gain[...] + bias[...]).astype(bf16)
    rows[...] = normed
    cols = weight.shape[2]
    for s in range(3):
        lin[:, s * cols : (s + 1) * cols] = dot(normed, weight[s], NN)


def norm_qkv(x, tokens, weight, gain, bias):
    _, width, cols = weight.shape
    block = min(256, tokens)
    rows = pl.BlockSpec((block, width), lambda r: (r, 0))
    vector = pl.BlockSpec((1, width), lambda r: (0, 0))
    return pl.pallas_call(
        norm_qkv_kernel,
        grid=(tokens // block,),
        in_specs=[rows, pl.BlockSpec((3, width, cols), lambda r: (0, 0, 0)), vector, vector],
        out_specs=[rows, pl.BlockSpec((block, 3 * cols), lambda r: (r, 0))],
        out_shape=[
            jax.ShapeDtypeStruct((tokens, width), bf16),
            jax.ShapeDtypeStruct((tokens, 3 * cols), f32),
        ],
        compiler_params=pltpu.CompilerParams(vmem_limit_bytes=VMEM),
        cost_estimate=COST,
    )(x, weight, gain[None], bias[None])


def project_norm_kernel(att, weight, x, gain, bias, mid, rows, held, sem):
    dp_size, mp_size, part, _ = weight.shape

    @pl.when(pl.program_id(0) == 0)
    def _():
        for d in range(dp_size):
            for j in range(mp_size):
                target = held.at[pl.ds((j * dp_size + d) * part, part), :]
                pltpu.make_async_copy(weight.at[d, j], target, sem).start()
        pltpu.make_async_copy(held, held, sem).wait()

    v = x[...].astype(f32) + dot(att[...], held[...], NN)
    mid[...] = v
    centred = v - jnp.mean(v, axis=1, keepdims=True)
    rstd = lax.rsqrt(jnp.mean(centred * centred, axis=1, keepdims=True) + EPSILON)
    rows[...] = (centred * rstd * gain[...] + bias[...]).astype(bf16)


def project_norm(att, weight, x, gain, bias):
    tokens, width = att.shape
    block = min(256, tokens)
    rows = pl.BlockSpec((block, width), lambda r: (r, 0))
    vector = pl.BlockSpec((1, width), lambda r: (0, 0))
    return pl.pallas_call(
        project_norm_kernel,
        grid=(tokens // block,),
        in_specs=[rows, pl.BlockSpec(memory_space=pl.ANY), rows, vector, vector],
        out_specs=[rows, rows],
        out_shape=[
            jax.ShapeDtypeStruct((tokens, width), f32),
            jax.ShapeDtypeStruct((tokens, width), bf16),
        ],
        scratch_shapes=[pltpu.VMEM((width, width), bf16), pltpu.SemaphoreType.DMA(())],
        compiler_params=pltpu.CompilerParams(vmem_limit_bytes=VMEM),
        cost_estimate=COST,
    )(att, weight, x, gain[None], bias[None])


def add_rows(vec, *arrays):
    @pl.when(pl.program_id(0) == 0)
    def _():
        vec[...] = jnp.zeros_like(vec)

    for i, a in enumerate(arrays):
        vec[i : i + 1, :] += jnp.sum(a, axis=0, keepdims=True)


def attn_in_backward_kernel(g, weight, x, gain, low, plain, cross, vec):
    cols = weight.shape[2]
    part = sum(dot(g[:, s * cols : (s + 1) * cols], weight[s], NT) for s in range(3))
    low[...] = part.astype(bf16)
    v = x[...].astype(f32)
    centred = v - jnp.mean(v, axis=1, keepdims=True)
    xhat = centred * lax.rsqrt(jnp.mean(centred * centred, axis=1, keepdims=True) + EPSILON)
    crossed = part * xhat
    plain[...] = jnp.sum(part * gain[...], axis=1, keepdims=True)
    cross[...] = jnp.sum(crossed * gain[...], axis=1, keepdims=True)
    add_rows(vec, crossed, part)


def attn_in_backward(g_rows, weight, x, gain):
    tokens, wide = g_rows.shape
    width, cols = weight.shape[1:]
    block = min(256, tokens)
    rows = pl.BlockSpec((block, width), lambda r: (r, 0))
    column = pl.BlockSpec((block, 1), lambda r: (r, 0))
    return pl.pallas_call(
        attn_in_backward_kernel,
        grid=(tokens // block,),
        in_specs=[
            pl.BlockSpec((block, wide), lambda r: (r, 0)),
            pl.BlockSpec((3, width, cols), lambda r: (0, 0, 0)),
            rows,
            pl.BlockSpec((1, width), lambda r: (0, 0)),
        ],
        out_specs=[rows, column, column, pl.BlockSpec((2, width), lambda r: (0, 0))],
        out_shape=[
            jax.ShapeDtypeStruct((tokens, width), bf16),
            jax.ShapeDtypeStruct((tokens, 1), f32),
            jax.ShapeDtypeStruct((tokens, 1), f32),
            jax.ShapeDtypeStruct((2, width), f32),
        ],
        compiler_params=pltpu.CompilerParams(vmem_limit_bytes=VMEM),
        cost_estimate=COST,
    )(g_rows, weight, x, gain[None])


def mid_backward_kernel(me, g_ffn, gy, mid, gain, low, mine, vec):
    v = mid[...]
    centred = v - jnp.mean(v, axis=1, keepdims=True)
    rstd = lax.rsqrt(jnp.mean(centred * centred, axis=1, keepdims=True) + EPSILON)
    xhat = centred * rstd
    grad_normed = g_ffn[...].astype(f32)
    add_rows(vec, grad_normed * xhat, grad_normed)
    scaled = grad_normed * gain[...]
    plain = jnp.mean(scaled, axis=1, keepdims=True)
    cross = jnp.mean(scaled * xhat, axis=1, keepdims=True)
    grad = gy[...].astype(f32) + rstd * (scaled - plain - xhat * cross)
    low[...] = grad.astype(bf16)
    cols = mine.shape[1]
    for j in range(grad.shape[1] // cols):

        @pl.when(me[0] == j)
        def _(j=j):
            mine[...] = grad[:, j * cols : (j + 1) * cols]


def mid_backward(g_ffn, gy, mid, gain):
    tokens, width = mid.shape
    feats = width // lax.axis_size("mp")
    block = min(128, tokens)
    rows = pl.BlockSpec((block, width), lambda r, me: (r, 0))
    return pl.pallas_call(
        mid_backward_kernel,
        grid_spec=pltpu.PrefetchScalarGridSpec(
            num_scalar_prefetch=1,
            grid=(tokens // block,),
            in_specs=[rows, rows, rows, pl.BlockSpec((1, width), lambda r, me: (0, 0))],
            out_specs=[
                rows,
                pl.BlockSpec((block, feats), lambda r, me: (r, 0)),
                pl.BlockSpec((2, width), lambda r, me: (0, 0)),
            ],
        ),
        out_shape=[
            jax.ShapeDtypeStruct((tokens, width), bf16),
            jax.ShapeDtypeStruct((tokens, feats), f32),
            jax.ShapeDtypeStruct((2, width), f32),
        ],
        compiler_params=pltpu.CompilerParams(vmem_limit_bytes=VMEM),
        cost_estimate=COST,
    )(lax.axis_index("mp").reshape(1).astype(jnp.int32), g_ffn, gy, mid, gain[None])


def split_bits(v):
    high = lax.reduce_precision(v, 8, 7)
    return [high.astype(bf16), (v - high).astype(bf16)]


def normalize(v):
    mean = jnp.mean(v, axis=1, keepdims=True)
    centred = v - mean
    rstd = lax.rsqrt(jnp.mean(centred * centred, axis=1, keepdims=True) + EPSILON)
    return centred * rstd, rstd


def local(
    inputs,
    segment_ids,
    width_bucket,
    attn_gain,
    attn_bias,
    qkv_weight,
    proj_weight,
    ffn_gain,
    ffn_bias,
    up_weight,
    down_weight,
    grad_result,
):
    tokens, feats = inputs.shape
    row_len = segment_ids.shape[1]
    mp_size = lax.axis_size("mp")
    dp_size = lax.axis_size("dp")
    mp_idx = lax.axis_index("mp")
    width = feats * mp_size

    def own(a):
        return lax.dynamic_slice_in_dim(a, mp_idx * feats, feats, a.ndim - 1)

    half = HEAD_DIM // 2
    freqs = jnp.power(10000.0, -jnp.arange(half, dtype=f32) / half)
    angles = jnp.arange(row_len, dtype=f32)[:, None] * freqs[None, :]
    cos_h, sin_h = jnp.cos(angles), jnp.sin(angles)
    cos_t = jnp.concatenate([cos_h, cos_h], axis=1)
    sin_t = jnp.concatenate([-sin_h, sin_h], axis=1)

    vectors = sum((split_bits(v) for v in (attn_gain, attn_bias, ffn_gain, ffn_bias)), [])
    packed = jnp.concatenate([jnp.stack(vectors), jnp.zeros((8, feats), bf16)])
    first, second = split_rows(inputs)
    chunks = [first, jnp.concatenate([second, packed])]
    starts = [line_step(1, c, c) for c in chunks]
    parts = [line_parts(c, pair) for c, pair in zip(chunks, starts)]
    gy_own = after(grad_result, *(p[1][min(1, mp_size - 2)] for p in parts))
    gathered = join(parts)
    vec = gathered[tokens : tokens + 8].astype(f32)
    gain_a, bias_a, gain_f, bias_f = (vec[2 * i] + vec[2 * i + 1] for i in range(4))
    gy_steps = [line_step(1, gy_own, gy_own)]

    part = proj_weight.shape[0] // dp_size
    slab = lax.dynamic_slice_in_dim(proj_weight, lax.axis_index("dp") * part, part, 0)
    slab = lax.all_gather(after(slab, gathered), "mp", axis=0)
    attn_rows, lin = norm_qkv(gathered, tokens, qkv_weight, gain_a, bias_a)
    att, rot = attn_forward(lin, cos_t, sin_t, segment_ids)
    att, slab, gy_steps[0] = lax.optimization_barrier((att, slab, gy_steps[0]))
    proj_full = lax.all_gather(slab, "dp", axis=0)
    att_full, proj_full = lax.optimization_barrier((line_gather(split_rows(att)), proj_full))
    gy_steps[0] = tuple(after(a, att_full) for a in gy_steps[0])
    gy_steps.append(line_step(2, *gy_steps[0]))
    mid, ffn_rows = project_norm(att_full, proj_full, gathered, gain_f, bias_f)
    ffn_rows, gy_steps[1] = lax.optimization_barrier((ffn_rows, gy_steps[1]))
    for s in range(3, mp_size):
        gy_steps.append(line_step(s, *gy_steps[-1]))

    limit = (width_bucket.reshape(tokens) + 1) * (FF // 4)
    columns = mp_idx * up_weight.shape[1] + jnp.arange(up_weight.shape[1], dtype=jnp.int32)
    keep = columns[None, :] < limit[:, None]
    hidden = dot(ffn_rows, up_weight, NN)
    relu = jnp.where(keep, jnp.maximum(hidden, 0.0), 0.0)
    active = (relu * relu).astype(bf16)

    gy = join([(gy_own, [r for r, _ in gy_steps], [l for _, l in gy_steps])])
    gy, active, relu = lax.optimization_barrier((gy, active, relu))
    grad_hidden = (2.0 * relu * dot(gy, down_weight, NT)).astype(bf16)
    g_ffn_part = dot(grad_hidden, up_weight, NT).astype(bf16)
    g_ffn_own = lax.psum_scatter(g_ffn_part, "mp", scatter_dimension=1, tiled=True)

    active, gy = (after(a, g_ffn_part) for a in (active, gy))
    down = Halving(lambda half: dot(half_lanes(active, half), gy, TN).astype(bf16))
    grad_up = dot(after(ffn_rows, down.x), grad_hidden, TN).astype(bf16)
    (grad_up,) = meet((grad_up,), down)
    grad_up = lax.psum_scatter(grad_up, "dp", scatter_dimension=0, tiled=True)
    ffn_part = dot(after(active, down.x), down_weight, NN).astype(bf16)
    down.x = after(down.x, ffn_part)
    g_ffn_own, ffn_part = meet((g_ffn_own, ffn_part), down)
    chunks = split_rows(g_ffn_own)
    starts = [line_step(1, c, c) for c in chunks]
    starts[0] = meet(starts[0], down)
    g_ffn = join([line_parts(c, pair) for c, pair in zip(chunks, starts)])
    up = Pieces(grad_up, lambda device: device, dp_rounds())
    g_ffn, ffn_part = meet((g_ffn, ffn_part), up, down)
    ffn_out = lax.psum_scatter(ffn_part, "mp", scatter_dimension=1, tiled=True)

    grad_mid_low, grad_mid_own, ffn_vec = mid_backward(g_ffn, gy, mid, gain_f)
    g_att = dot(grad_mid_low, proj_weight, NT).astype(bf16)
    g_qkv_rows = attn_backward(rot, g_att, cos_t, sin_t, segment_ids)
    (g_qkv_rows,) = meet((g_qkv_rows,), down, up)
    qkv = Halving(lambda half: dot(half_lanes(attn_rows, half), g_qkv_rows, TN).astype(bf16))
    (later,) = meet((g_qkv_rows,), qkv)
    g_attn_low, plain, cross, attn_vec = attn_in_backward(later, qkv_weight, gathered, gain_a)
    g_attn = lax.psum_scatter(g_attn_low, "mp", scatter_dimension=1, tiled=True).astype(f32)

    mid_later, _, ffn_out = meet((grad_mid_low, g_attn_low, ffn_out), down, up)
    proj = Halving(lambda half: dot(half_lanes(att, half), mid_later, TN).astype(bf16))
    proj.x = meet(proj.x, qkv, up)
    down.x = after(down.x, proj.x)
    (grad_down,) = meet((down.finish()[0],), qkv, proj)
    up.x = after(up.x, grad_down)
    (grad_up,) = meet((up.finish()[0],), qkv, proj)
    sums = jnp.concatenate([attn_vec, jnp.stack([plain, cross]).reshape(-1, width)])
    sums = butterfly_sum(sums, "mp")
    sum_plain, sum_cross = sums[2:].reshape(2, tokens, 1)
    vec = jnp.concatenate([own(sums[:2]), own(ffn_vec)])
    vec, sum_plain, g_attn = meet((vec, sum_plain, g_attn), qkv, proj)
    grad_vec = butterfly_sum(vec, "dp")
    grad_qkv, grad_proj = qkv.finish(3), proj.finish()[0]

    ffn_out = ffn_out.astype(f32)
    xhat_a, rstd_a = normalize(after(gathered, grad_up)[:tokens].astype(f32))
    grad_input = grad_mid_own + rstd_a * (
        g_attn * attn_gain - sum_plain / width - own(xhat_a) * (sum_cross / width)
    )
    block_output = (own(mid) + ffn_out).astype(bf16)
    return (
        block_output,
        grad_input,
        grad_vec[0],
        grad_vec[1],
        grad_qkv,
        grad_proj,
        grad_vec[2],
        grad_vec[3],
        grad_up,
        grad_down,
    )


def solution(mesh):
    placed = (
        P("dp", "mp"),
        P("dp", None),
        P("dp", None),
        P("mp"),
        P("mp"),
        P(None, None, "mp"),
        P("mp", None),
        P("mp"),
        P("mp"),
        P(None, "mp"),
        P("mp", None),
        P("dp", "mp"),
    )
    return jax.shard_map(
        local,
        mesh=mesh,
        in_specs=placed,
        out_specs=(
            P("dp", "mp"),
            P("dp", "mp"),
            P("mp"),
            P("mp"),
            P(None, None, "mp"),
            P("mp", None),
            P("mp"),
            P("mp"),
            P(None, "mp"),
            P("mp", None),
        ),
        check_vma=False,
    )
```

```python
import functools

import jax
import jax.numpy as jnp
from jax import lax
from jax.experimental import pallas as pl
from jax.experimental.pallas import tpu as pltpu
from jax.sharding import PartitionSpec as P

HEAD_DIM = 128
FF = 8192
EPSILON = 1e-05
MASKED = -1e30
LONGEST_DOC = 512
QUERY_BLOCK = 256
VMEM = 36 * 2**20
COST = pl.CostEstimate(flops=1, bytes_accessed=1, transcendentals=0)

bf16 = jnp.bfloat16
f32 = jnp.float32

NT = (((1,), (1,)), ((), ()))
TN = (((0,), (0,)), ((), ()))
NN = (((1,), (0,)), ((), ()))


def dot(a, b, dims):
    return lax.dot_general(a, b, dims, preferred_element_type=f32)


def block_probs(i, rot, seg_row, seg_col, block, scale):
    start = i * block
    low = max(0, start - LONGEST_DOC)
    high = start + block
    q = rot[0, start:high, :]
    k = rot[1, low:high, :]
    scores = dot(q, k, NT) * scale
    shape = scores.shape
    q_pos = start + lax.broadcasted_iota(jnp.int32, shape, 0)
    k_pos = low + lax.broadcasted_iota(jnp.int32, shape, 1)
    allowed = (seg_col[start:high, :] == seg_row[0][:, low:high]) & (k_pos <= q_pos)
    scores = jnp.where(allowed, scores, MASKED)
    expo = jnp.exp(scores - jnp.max(scores, axis=1, keepdims=True))
    return expo * (1.0 / jnp.sum(expo, axis=1, keepdims=True)), q, k, start, low, high


def attn_fwd_kernel(block, scale, q_lin, k_lin, v_lin, cosine, sine, seg_row, seg_col, att, rot):
    cos_t = cosine[...]
    sin_t = sine[...]
    for s, lin in ((0, q_lin), (1, k_lin)):
        z = lin[...]
        rot[s] = (z * cos_t + pltpu.roll(z, HEAD_DIM // 2, 1) * sin_t).astype(bf16)
    rot[2] = v_lin[...].astype(bf16)
    for i in range(q_lin.shape[0] // block):
        probs, _, _, start, low, high = block_probs(i, rot, seg_row, seg_col, block, scale)
        att[start:high, :] = dot(probs.astype(bf16), rot[2, low:high, :], NN).astype(bf16)


def attn_bwd_kernel(block, scale, rot, g_att, cosine, sine, seg_row, seg_col, grads, dk, dv):
    cos_t = cosine[...]
    sin_t = sine[...]
    cols = grads.shape[1] // 3
    at = pl.program_id(1) * HEAD_DIM
    dk[...] = jnp.zeros_like(dk)
    dv[...] = jnp.zeros_like(dv)

    def lanes(s):
        return pl.ds(pl.multiple_of(s * cols + at, HEAD_DIM), HEAD_DIM)

    def back(z, c, s):
        return (z * c - pltpu.roll(z, HEAD_DIM // 2, 1) * s).astype(bf16)

    for i in range(rot.shape[1] // block):
        probs, q, k, start, low, high = block_probs(i, rot, seg_row, seg_col, block, scale)
        g = g_att[start:high, :]
        g_probs = dot(g, rot[2, low:high, :], NT)
        delta = jnp.sum(probs * g_probs, axis=1, keepdims=True)
        g_raw = (probs * (g_probs - delta) * scale).astype(bf16)
        grads[start:high, lanes(0)] = back(
            dot(g_raw, k, NN), cos_t[start:high, :], sin_t[start:high, :]
        )
        dk[low:high, :] += dot(g_raw, q, TN)
        dv[low:high, :] += dot(probs.astype(bf16), g, TN)
    grads[:, lanes(1)] = back(dk[...], cos_t, sin_t)
    grads[:, lanes(2)] = dv[...].astype(bf16)


def attention_specs(row_len):
    triple = pl.BlockSpec((3, row_len, HEAD_DIM), lambda r, h: (0, r, h))
    plain = pl.BlockSpec((row_len, HEAD_DIM), lambda r, h: (r, h))
    table = pl.BlockSpec((row_len, HEAD_DIM), lambda r, h: (0, 0))
    seg_row = pl.BlockSpec((1, 1, row_len), lambda r, h: (r, 0, 0))
    seg_col = pl.BlockSpec((row_len, 1), lambda r, h: (r, 0))
    return triple, plain, table, seg_row, seg_col


def attn_forward(lin, cos_t, sin_t, segs, seg_col):
    tokens = lin.shape[0]
    cols = lin.shape[1] // 3
    heads = cols // HEAD_DIM
    rows, row_len = segs.shape
    triple, plain, table, row_spec, col_spec = attention_specs(row_len)
    block = min(QUERY_BLOCK, row_len)
    parts = [
        pl.BlockSpec((row_len, HEAD_DIM), lambda r, h, s=s: (r, s * heads + h)) for s in range(3)
    ]
    return pl.pallas_call(
        functools.partial(attn_fwd_kernel, block, HEAD_DIM**-0.5),
        grid=(rows, heads),
        in_specs=[*parts, table, table, row_spec, col_spec],
        out_specs=[plain, triple],
        out_shape=[
            jax.ShapeDtypeStruct((tokens, cols), bf16),
            jax.ShapeDtypeStruct((3, tokens, cols), bf16),
        ],
        compiler_params=pltpu.CompilerParams(vmem_limit_bytes=VMEM),
        cost_estimate=COST,
    )(lin, lin, lin, cos_t, sin_t, segs[:, None, :], seg_col)


def attn_backward(rot, g_att, cos_t, sin_t, segs, seg_col):
    _, tokens, cols = rot.shape
    rows, row_len = segs.shape
    triple, plain, table, row_spec, col_spec = attention_specs(row_len)
    block = min(QUERY_BLOCK, row_len)
    return pl.pallas_call(
        functools.partial(attn_bwd_kernel, block, HEAD_DIM**-0.5),
        grid=(rows, cols // HEAD_DIM),
        in_specs=[triple, plain, table, table, row_spec, col_spec],
        out_specs=pl.BlockSpec((row_len, 3 * cols), lambda r, h: (r, 0)),
        out_shape=jax.ShapeDtypeStruct((tokens, 3 * cols), bf16),
        scratch_shapes=[pltpu.VMEM((row_len, HEAD_DIM), f32)] * 2,
        compiler_params=pltpu.CompilerParams(vmem_limit_bytes=VMEM),
        cost_estimate=COST,
    )(rot, g_att, cos_t, sin_t, segs[:, None, :], seg_col)


def after(value, *deps):
    return lax.optimization_barrier((value,) + deps)[0]


def join_kernel(n, chunks, *refs):
    per = 2 * n - 1
    out, sem = refs[chunks * per], refs[chunks * per + 1]
    me = lax.axis_index("mp")
    at = 0
    for c in range(chunks):
        own, right, left = refs[c * per], refs[c * per + 1 : c * per + n], refs[c * per + n : c * per + per]
        rows, cols = own.shape

        def put(src, block, at=at, rows=rows, cols=cols):
            target = out.at[
                pl.ds(at, rows), pl.ds(pl.multiple_of(block * cols, cols), cols)
            ]
            pltpu.make_async_copy(src, target, sem).start()

        at += rows
        put(own, me)
        for s in range(1, n):
            pl.when(me >= s)(functools.partial(put, right[s - 1], me - s))
            pl.when(me + s < n)(functools.partial(put, left[s - 1], me + s))
    pltpu.make_async_copy(out, out, sem).wait()


def join(parts):
    n = lax.axis_size("mp")
    rows = sum(p[0].shape[0] for p in parts)
    flat = [a for own, right, left in parts for a in (own, *right, *left)]
    shape = (rows, n * parts[0][0].shape[1])
    return pl.pallas_call(
        functools.partial(join_kernel, n, len(parts)),
        in_specs=[pl.BlockSpec(memory_space=pl.ANY)] * len(flat),
        out_specs=pl.BlockSpec(memory_space=pltpu.VMEM),
        out_shape=jax.ShapeDtypeStruct(shape, parts[0][0].dtype),
        scratch_shapes=[pltpu.SemaphoreType.DMA(())],
        compiler_params=pltpu.CompilerParams(vmem_limit_bytes=VMEM),
        cost_estimate=COST,
    )(*flat)


def line_step(s, right, left):
    n = lax.axis_size("mp")
    return (
        lax.ppermute(right, "mp", [(i, i + 1) for i in range(s - 1, n - 1)]),
        lax.ppermute(left, "mp", [(i, i - 1) for i in range(1, n - s + 1)]),
    )


def line_parts(block, first=None):
    right = left = block
    rights, lefts = [], []
    for s in range(1, lax.axis_size("mp")):
        if s == 1 and first is not None:
            right, left = first
        else:
            right, left = line_step(s, right, left)
        rights.append(right)
        lefts.append(left)
    return block, rights, lefts


def line_gather(chunks):
    return join([line_parts(c) for c in chunks])


def split_rows(x, chunks=2):
    return jnp.split(x, chunks, axis=0)


class Scatter:
    def __init__(self, y):
        self.n = lax.axis_size("mp")
        self.me = lax.axis_index("mp")
        self.y = y
        self.step = 0
        self.x = (self.block(self.n - 1), self.block(1 - self.n))
        self.flight = None
        self.launch()

    def block(self, offset):
        cols = self.y.shape[1] // self.n
        at = jnp.clip(self.me + offset, 0, self.n - 1) * cols
        return lax.dynamic_slice_in_dim(self.y, at, cols, 1)

    def launch(self):
        self.step += 1
        n, s = self.n, self.step
        if s < n:
            right, left = self.x
            self.flight = (
                lax.ppermute(right, "mp", [(i, i + 1) for i in range(s)]),
                lax.ppermute(left, "mp", [(i, i - 1) for i in range(n - s, n)]),
            )

    def land(self):
        if self.flight is not None:
            ahead = self.n - self.step - 1
            self.x = self.flight
            if ahead > 0:
                self.x = tuple(
                    (a.astype(f32) + self.block(offset).astype(f32)).astype(bf16)
                    for a, offset in zip(self.x, (ahead, -ahead))
                )
            self.flight = None

    def finish(self):
        while self.flight is not None:
            self.land()
            self.launch()
        return sum(a.astype(f32) for a in (*self.x, self.block(0)))


def dp_pairs(bits):
    return [(i, i ^ (1 << bits[i & 1])) for i in range(lax.axis_size("dp"))]


def dp_rounds():
    rest = list(range(1, lax.axis_size("dp").bit_length() - 1))
    return list(zip(rest, rest[1:] + rest[:1]))


def by_parity(odd, bits, value):
    return jnp.where(odd == 1, value(bits[1]), value(bits[0]))


class Pieces:
    def __init__(self, piece, place, rounds):
        self.x = (piece,)
        self.flight = None
        self.me = lax.axis_index("dp")
        self.owners = [self.me]
        self.place = place
        self.rounds = list(reversed(rounds))
        self.todo = self.rounds + [(0, 0)]

    def launch(self):
        if self.todo and self.flight is None:
            bits = self.todo.pop(0)
            if self.todo and len(self.x) > 1:
                self.x = (jnp.concatenate(self.x),)
            got = tuple(lax.ppermute(p, "dp", dp_pairs(bits)) for p in self.x)
            self.flight = (bits, got)

    def land(self):
        if self.flight is None:
            return
        bits, got = self.flight
        self.flight = None
        self.x = self.x + got
        if self.todo:
            flip = by_parity(self.me & 1, bits, lambda b: 1 << b)
            self.owners = self.owners + [o ^ flip for o in self.owners]
        else:
            theirs = [self.me ^ 1]
            for bits in self.rounds:
                flip = by_parity(1 - (self.me & 1), bits, lambda b: 1 << b)
                theirs = theirs + [o ^ flip for o in theirs]
            self.owners = self.owners + theirs

    def finish(self, groups=1):
        while self.todo or self.flight is not None:
            self.land()
            self.launch()
        return widen(self.x, jnp.stack([self.place(o) for o in self.owners]), groups)


class Halving:
    def __init__(self, make, whole=False):
        self.me = lax.axis_index("dp")
        odd = self.me & 1
        self.todo = dp_rounds()
        self.whole = whole
        self.pieces = None
        sent = make(1 - odd)
        self.x = (make(after(odd, sent)),)
        self.flight = lax.ppermute(sent, "dp", dp_pairs((0, 0)))

    def place(self, device):
        odd = device & 1
        at = odd
        if not self.whole:
            for bits in dp_rounds():
                at = at * 2 + by_parity(odd, bits, lambda b: (device >> b) & 1)
        return at

    def launch(self):
        if self.pieces is not None:
            self.pieces.x = self.x
            self.pieces.launch()
        elif self.todo and self.flight is None:
            bits = self.todo.pop(0)
            *kept, sent = self.x
            self.x = tuple(kept) or (sent,)
            self.flight = lax.ppermute(sent, "dp", dp_pairs(bits))

    def land(self):
        if self.pieces is not None:
            self.pieces.land()
            self.x = self.pieces.x
        elif self.flight is not None:
            (kept,) = self.x
            got = self.flight
            self.flight = None

            def add(at=0, rows=kept.shape[0]):
                terms = (lax.dynamic_slice_in_dim(a, at, rows, 0) for a in (kept, got))
                return sum(a.astype(f32) for a in terms).astype(bf16)

            if not self.todo:
                self.x = (add(),)
                rounds = [] if self.whole else dp_rounds()
                self.pieces = Pieces(self.x[0], self.place, rounds)
            elif self.whole:
                self.x = (add(),)
            else:
                half = kept.shape[0] // 2
                bit = by_parity(self.me & 1, self.todo[0], lambda b: (self.me >> b) & 1)
                self.x = (add(bit * half, half), add((1 - bit) * half, half))

    def finish(self, groups=1):
        while self.pieces is None:
            self.land()
            self.launch()
        self.pieces.x = self.x
        return self.pieces.finish(groups)


def widen_kernel(firsts, table, *refs):
    *arrays, out = refs
    groups, _, cols = out.shape
    step = pl.program_id(0)
    for k, src in enumerate(arrays):

        @pl.when((step >= firsts[k]) & (step < firsts[k + 1]))
        def _(src=src):
            for g in range(groups):
                out[g] = src[:, g * cols : (g + 1) * cols].astype(f32)


def widen(arrays, places, groups):
    total = sum(a.shape[0] for a in arrays)
    cols = arrays[0].shape[1]
    rows = total // places.shape[0]
    block = min(256, rows)
    per = rows // block
    wide = cols // groups
    firsts = [sum(a.shape[0] for a in arrays[:k]) // block for k in range(len(arrays) + 1)]

    def spec(k):
        def index(step, table):
            return (jnp.clip(step - firsts[k], 0, firsts[k + 1] - firsts[k] - 1), 0)

        return pl.BlockSpec((block, cols), index)

    def out_index(step, table):
        return (0, table[step // per] * per + step % per, 0)

    return pl.pallas_call(
        functools.partial(widen_kernel, firsts),
        grid_spec=pltpu.PrefetchScalarGridSpec(
            num_scalar_prefetch=1,
            grid=(total // block,),
            in_specs=[spec(k) for k in range(len(arrays))],
            out_specs=pl.BlockSpec((groups, block, wide), out_index),
        ),
        out_shape=jax.ShapeDtypeStruct((groups, total, wide), f32),
        compiler_params=pltpu.CompilerParams(vmem_limit_bytes=VMEM),
        cost_estimate=COST,
    )(places.astype(jnp.int32), *arrays)


def half_lanes(x, half):
    size = x.shape[1] // 2
    return lax.dynamic_slice_in_dim(x, half * size, size, 1)


def meet(values, *sums):
    for h in sums:
        h.land()
    met, xs = lax.optimization_barrier((tuple(values), tuple(h.x for h in sums)))
    for h, x in zip(sums, xs):
        h.x = x
        h.launch()
    return met


def butterfly_sum(x, axis):
    size = lax.axis_size(axis)
    for bit in range(size.bit_length() - 1):
        x = x + lax.ppermute(x, axis, [(i, i ^ (1 << bit)) for i in range(size)])
    return x


def norm_qkv_kernel(x, weight, gain, bias, rows, lin):
    v = x[...].astype(f32)
    centred = v - jnp.mean(v, axis=1, keepdims=True)
    rstd = lax.rsqrt(jnp.mean(centred * centred, axis=1, keepdims=True) + EPSILON)
    normed = (centred * rstd * gain[...] + bias[...]).astype(bf16)
    rows[...] = normed
    cols = weight.shape[2]
    for s in range(3):
        lin[:, s * cols : (s + 1) * cols] = dot(normed, weight[s], NN)


def norm_qkv(x, tokens, weight, gain, bias):
    _, width, cols = weight.shape
    block = min(256, tokens)
    rows = pl.BlockSpec((block, width), lambda r: (r, 0))
    vector = pl.BlockSpec((1, width), lambda r: (0, 0))
    return pl.pallas_call(
        norm_qkv_kernel,
        grid=(tokens // block,),
        in_specs=[rows, pl.BlockSpec((3, width, cols), lambda r: (0, 0, 0)), vector, vector],
        out_specs=[rows, pl.BlockSpec((block, 3 * cols), lambda r: (r, 0))],
        out_shape=[
            jax.ShapeDtypeStruct((tokens, width), bf16),
            jax.ShapeDtypeStruct((tokens, 3 * cols), f32),
        ],
        compiler_params=pltpu.CompilerParams(vmem_limit_bytes=VMEM),
        cost_estimate=COST,
    )(x, weight, gain[None], bias[None])


def project_norm_kernel(att, weight, x, gain, bias, mid, rows, held, sem):
    dp_size, mp_size, part, _ = weight.shape

    @pl.when(pl.program_id(0) == 0)
    def _():
        for d in range(dp_size):
            for j in range(mp_size):
                target = held.at[pl.ds((j * dp_size + d) * part, part), :]
                pltpu.make_async_copy(weight.at[d, j], target, sem).start()
        pltpu.make_async_copy(held, held, sem).wait()

    v = x[...].astype(f32) + dot(att[...], held[...], NN)
    mid[...] = v
    centred = v - jnp.mean(v, axis=1, keepdims=True)
    rstd = lax.rsqrt(jnp.mean(centred * centred, axis=1, keepdims=True) + EPSILON)
    rows[...] = (centred * rstd * gain[...] + bias[...]).astype(bf16)


def project_norm(att, weight, x, gain, bias):
    tokens, width = att.shape
    block = min(256, tokens)
    rows = pl.BlockSpec((block, width), lambda r: (r, 0))
    vector = pl.BlockSpec((1, width), lambda r: (0, 0))
    return pl.pallas_call(
        project_norm_kernel,
        grid=(tokens // block,),
        in_specs=[rows, pl.BlockSpec(memory_space=pl.ANY), rows, vector, vector],
        out_specs=[rows, rows],
        out_shape=[
            jax.ShapeDtypeStruct((tokens, width), f32),
            jax.ShapeDtypeStruct((tokens, width), bf16),
        ],
        scratch_shapes=[pltpu.VMEM((width, width), bf16), pltpu.SemaphoreType.DMA(())],
        compiler_params=pltpu.CompilerParams(vmem_limit_bytes=VMEM),
        cost_estimate=COST,
    )(att, weight, x, gain[None], bias[None])


def add_rows(vec, *arrays):
    @pl.when(pl.program_id(0) == 0)
    def _():
        vec[...] = jnp.zeros_like(vec)

    for i, a in enumerate(arrays):
        vec[i : i + 1, :] += jnp.sum(a, axis=0, keepdims=True)


def attn_in_backward_kernel(g, weight, x, gain, low, plain, cross, vec):
    cols = weight.shape[2]
    part = sum(dot(g[:, s * cols : (s + 1) * cols], weight[s], NT) for s in range(3))
    low[...] = part.astype(bf16)
    v = x[...].astype(f32)
    centred = v - jnp.mean(v, axis=1, keepdims=True)
    xhat = centred * lax.rsqrt(jnp.mean(centred * centred, axis=1, keepdims=True) + EPSILON)
    crossed = part * xhat
    plain[...] = jnp.sum(part * gain[...], axis=1, keepdims=True)
    cross[...] = jnp.sum(crossed * gain[...], axis=1, keepdims=True)
    add_rows(vec, crossed, part)


def attn_in_backward(g_rows, weight, x, gain):
    tokens, wide = g_rows.shape
    width, cols = weight.shape[1:]
    block = min(256, tokens)
    rows = pl.BlockSpec((block, width), lambda r: (r, 0))
    column = pl.BlockSpec((block, 1), lambda r: (r, 0))
    return pl.pallas_call(
        attn_in_backward_kernel,
        grid=(tokens // block,),
        in_specs=[
            pl.BlockSpec((block, wide), lambda r: (r, 0)),
            pl.BlockSpec((3, width, cols), lambda r: (0, 0, 0)),
            rows,
            pl.BlockSpec((1, width), lambda r: (0, 0)),
        ],
        out_specs=[rows, column, column, pl.BlockSpec((2, width), lambda r: (0, 0))],
        out_shape=[
            jax.ShapeDtypeStruct((tokens, width), bf16),
            jax.ShapeDtypeStruct((tokens, 1), f32),
            jax.ShapeDtypeStruct((tokens, 1), f32),
            jax.ShapeDtypeStruct((2, width), f32),
        ],
        compiler_params=pltpu.CompilerParams(vmem_limit_bytes=VMEM),
        cost_estimate=COST,
    )(g_rows, weight, x, gain[None])


def mid_backward_kernel(me, g_ffn, gy, mid, gain, low, mine, vec):
    v = mid[...]
    centred = v - jnp.mean(v, axis=1, keepdims=True)
    rstd = lax.rsqrt(jnp.mean(centred * centred, axis=1, keepdims=True) + EPSILON)
    xhat = centred * rstd
    grad_normed = g_ffn[...].astype(f32)
    add_rows(vec, grad_normed * xhat, grad_normed)
    scaled = grad_normed * gain[...]
    plain = jnp.mean(scaled, axis=1, keepdims=True)
    cross = jnp.mean(scaled * xhat, axis=1, keepdims=True)
    grad = gy[...].astype(f32) + rstd * (scaled - plain - xhat * cross)
    low[...] = grad.astype(bf16)
    cols = mine.shape[1]
    for j in range(grad.shape[1] // cols):

        @pl.when(me[0] == j)
        def _(j=j):
            mine[...] = grad[:, j * cols : (j + 1) * cols]


def mid_backward(g_ffn, gy, mid, gain):
    tokens, width = mid.shape
    feats = width // lax.axis_size("mp")
    block = min(128, tokens)
    rows = pl.BlockSpec((block, width), lambda r, me: (r, 0))
    return pl.pallas_call(
        mid_backward_kernel,
        grid_spec=pltpu.PrefetchScalarGridSpec(
            num_scalar_prefetch=1,
            grid=(tokens // block,),
            in_specs=[rows, rows, rows, pl.BlockSpec((1, width), lambda r, me: (0, 0))],
            out_specs=[
                rows,
                pl.BlockSpec((block, feats), lambda r, me: (r, 0)),
                pl.BlockSpec((2, width), lambda r, me: (0, 0)),
            ],
        ),
        out_shape=[
            jax.ShapeDtypeStruct((tokens, width), bf16),
            jax.ShapeDtypeStruct((tokens, feats), f32),
            jax.ShapeDtypeStruct((2, width), f32),
        ],
        compiler_params=pltpu.CompilerParams(vmem_limit_bytes=VMEM),
        cost_estimate=COST,
    )(lax.axis_index("mp").reshape(1).astype(jnp.int32), g_ffn, gy, mid, gain[None])


def split_bits(v):
    high = lax.reduce_precision(v, 8, 7)
    return [high.astype(bf16), (v - high).astype(bf16)]


def normalize(v):
    mean = jnp.mean(v, axis=1, keepdims=True)
    centred = v - mean
    rstd = lax.rsqrt(jnp.mean(centred * centred, axis=1, keepdims=True) + EPSILON)
    return centred * rstd, rstd


def local(
    inputs,
    segment_ids,
    width_bucket,
    attn_gain,
    attn_bias,
    qkv_weight,
    proj_weight,
    ffn_gain,
    ffn_bias,
    up_weight,
    down_weight,
    grad_result,
):
    tokens, feats = inputs.shape
    row_len = segment_ids.shape[1]
    mp_size = lax.axis_size("mp")
    dp_size = lax.axis_size("dp")
    mp_idx = lax.axis_index("mp")
    width = feats * mp_size

    def own(a):
        return lax.dynamic_slice_in_dim(a, mp_idx * feats, feats, a.ndim - 1)

    half = HEAD_DIM // 2
    freqs = jnp.power(10000.0, -jnp.arange(half, dtype=f32) / half)
    angles = jnp.arange(row_len, dtype=f32)[:, None] * freqs[None, :]
    cos_h, sin_h = jnp.cos(angles), jnp.sin(angles)
    cos_t = jnp.concatenate([cos_h, cos_h], axis=1)
    sin_t = jnp.concatenate([-sin_h, sin_h], axis=1)

    vectors = sum((split_bits(v) for v in (attn_gain, attn_bias, ffn_gain, ffn_bias)), [])
    packed = jnp.concatenate([jnp.stack(vectors), jnp.zeros((8, feats), bf16)])
    first, second = split_rows(inputs)
    chunks = [first, jnp.concatenate([second, packed])]
    starts = [line_step(1, c, c) for c in chunks]
    starts[0], cos_t, sin_t, seg_col = lax.optimization_barrier(
        (starts[0], cos_t, sin_t, segment_ids.reshape(tokens, 1))
    )
    parts = [line_parts(c, pair) for c, pair in zip(chunks, starts)]
    gy_own = after(grad_result, *(p[1][min(1, mp_size - 2)] for p in parts))
    gathered = join(parts)
    vec = gathered[tokens : tokens + 8].astype(f32)
    gain_a, bias_a, gain_f, bias_f = (vec[2 * i] + vec[2 * i + 1] for i in range(4))
    gy_steps = [line_step(1, gy_own, gy_own)]

    part = proj_weight.shape[0] // dp_size
    slab = lax.dynamic_slice_in_dim(proj_weight, lax.axis_index("dp") * part, part, 0)
    slab = lax.all_gather(after(slab, gathered), "mp", axis=0)
    attn_rows, lin = norm_qkv(gathered, tokens, qkv_weight, gain_a, bias_a)
    att, rot = attn_forward(lin, cos_t, sin_t, segment_ids, seg_col)
    att, slab, gy_steps[0] = lax.optimization_barrier((att, slab, gy_steps[0]))
    proj_full = lax.all_gather(slab, "dp", axis=0)
    att_full, proj_full = lax.optimization_barrier((line_gather(split_rows(att)), proj_full))
    gy_steps[0] = tuple(after(a, att_full) for a in gy_steps[0])
    gy_steps.append(line_step(2, *gy_steps[0]))
    mid, ffn_rows = project_norm(att_full, proj_full, gathered, gain_f, bias_f)
    ffn_rows, gy_steps[1] = lax.optimization_barrier((ffn_rows, gy_steps[1]))
    for s in range(3, mp_size):
        gy_steps.append(line_step(s, *gy_steps[-1]))

    limit = (width_bucket.reshape(tokens) + 1) * (FF // 4)
    columns = mp_idx * up_weight.shape[1] + jnp.arange(up_weight.shape[1], dtype=jnp.int32)
    keep = columns[None, :] < limit[:, None]
    hidden = dot(ffn_rows, up_weight, NN)
    relu = jnp.where(keep, jnp.maximum(hidden, 0.0), 0.0)
    active = (relu * relu).astype(bf16)

    gy = join([(gy_own, [r for r, _ in gy_steps], [l for _, l in gy_steps])])
    gy, active, relu = lax.optimization_barrier((gy, active, relu))
    grad_hidden = (2.0 * relu * dot(gy, down_weight, NT)).astype(bf16)
    g_ffn_part = dot(grad_hidden, up_weight, NT).astype(bf16)
    g_ffn_own = lax.psum_scatter(g_ffn_part, "mp", scatter_dimension=1, tiled=True)

    active, gy = (after(a, g_ffn_part) for a in (active, gy))
    down = Halving(lambda half: dot(half_lanes(active, half), gy, TN).astype(bf16))
    grad_up = dot(after(ffn_rows, down.x), grad_hidden, TN).astype(bf16)
    (grad_up,) = meet((grad_up,), down)
    grad_up = lax.psum_scatter(grad_up, "dp", scatter_dimension=0, tiled=True)
    ffn_part = dot(after(active, down.x), down_weight, NN).astype(bf16)
    down.x = after(down.x, ffn_part)
    g_ffn_own, ffn_part = meet((g_ffn_own, ffn_part), down)
    chunks = split_rows(g_ffn_own)
    starts = [line_step(1, c, c) for c in chunks]
    starts[0] = meet(starts[0], down)
    g_ffn = join([line_parts(c, pair) for c, pair in zip(chunks, starts)])
    up = Pieces(grad_up, lambda device: device, dp_rounds())
    g_ffn, ffn_part = meet((g_ffn, ffn_part), up, down)
    ffn_out = lax.psum_scatter(ffn_part, "mp", scatter_dimension=1, tiled=True)

    grad_mid_low, grad_mid_own, ffn_vec = mid_backward(g_ffn, gy, mid, gain_f)
    g_att = dot(grad_mid_low, proj_weight, NT).astype(bf16)
    g_qkv_rows = attn_backward(rot, g_att, cos_t, sin_t, segment_ids, seg_col)
    (g_qkv_rows,) = meet((g_qkv_rows,), down)
    qkv = Halving(lambda half: dot(half_lanes(attn_rows, half), g_qkv_rows, TN).astype(bf16))
    (later,) = meet((g_qkv_rows,), qkv, up)
    g_attn_low, plain, cross, attn_vec = attn_in_backward(later, qkv_weight, gathered, gain_a)
    g_attn = lax.psum_scatter(g_attn_low, "mp", scatter_dimension=1, tiled=True).astype(f32)

    mid_later, _, ffn_out = meet((grad_mid_low, g_attn_low, ffn_out), down)
    proj = Halving(lambda half: dot(half_lanes(att, half), mid_later, TN).astype(bf16))
    proj.x = meet(proj.x, qkv)
    down.x = after(down.x, proj.x)
    (grad_down,) = meet((down.finish()[0],), qkv, proj, up)
    (grad_down,) = meet((grad_down,), qkv, proj)
    up.x = after(up.x, grad_down)
    (grad_up,) = meet((up.finish()[0],), qkv, proj)
    sums = jnp.concatenate([attn_vec, jnp.stack([plain, cross]).reshape(-1, width)])
    sums = butterfly_sum(sums, "mp")
    sum_plain, sum_cross = sums[2:].reshape(2, tokens, 1)
    vec = jnp.concatenate([own(sums[:2]), own(ffn_vec)])
    vec, sum_plain, g_attn = meet((vec, sum_plain, g_attn), qkv, proj)
    grad_vec = butterfly_sum(vec, "dp")
    grad_qkv, grad_proj = qkv.finish(3), proj.finish()[0]

    ffn_out = ffn_out.astype(f32)
    xhat_a, rstd_a = normalize(after(gathered, grad_up)[:tokens].astype(f32))
    grad_input = grad_mid_own + rstd_a * (
        g_attn * attn_gain - sum_plain / width - own(xhat_a) * (sum_cross / width)
    )
    block_output = (own(mid) + ffn_out).astype(bf16)
    return (
        block_output,
        grad_input,
        grad_vec[0],
        grad_vec[1],
        grad_qkv,
        grad_proj,
        grad_vec[2],
        grad_vec[3],
        grad_up,
        grad_down,
    )


def solution(mesh):
    placed = (
        P("dp", "mp"),
        P("dp", None),
        P("dp", None),
        P("mp"),
        P("mp"),
        P(None, None, "mp"),
        P("mp", None),
        P("mp"),
        P("mp"),
        P(None, "mp"),
        P("mp", None),
        P("dp", "mp"),
    )
    return jax.shard_map(
        local,
        mesh=mesh,
        in_specs=placed,
        out_specs=(
            P("dp", "mp"),
            P("dp", "mp"),
            P("mp"),
            P("mp"),
            P(None, None, "mp"),
            P("mp", None),
            P("mp"),
            P("mp"),
            P(None, "mp"),
            P("mp", None),
        ),
        check_vma=False,
    )
```

```python
import functools

import jax
import jax.numpy as jnp
from jax import lax
from jax.experimental import pallas as pl
from jax.experimental.pallas import tpu as pltpu
from jax.sharding import PartitionSpec as P

HEAD_DIM = 128
FF = 8192
EPSILON = 1e-05
MASKED = -1e30
LONGEST_DOC = 512
QUERY_BLOCK = 256
VMEM = 36 * 2**20
COST = pl.CostEstimate(flops=1, bytes_accessed=1, transcendentals=0)

bf16 = jnp.bfloat16
f32 = jnp.float32

NT = (((1,), (1,)), ((), ()))
TN = (((0,), (0,)), ((), ()))
NN = (((1,), (0,)), ((), ()))


def dot(a, b, dims):
    return lax.dot_general(a, b, dims, preferred_element_type=f32)


def block_probs(i, rot, seg_row, seg_col, block, scale):
    start = i * block
    low = max(0, start - LONGEST_DOC)
    high = start + block
    q = rot[0, start:high, :]
    k = rot[1, low:high, :]
    scores = dot(q, k, NT) * scale
    shape = scores.shape
    q_pos = start + lax.broadcasted_iota(jnp.int32, shape, 0)
    k_pos = low + lax.broadcasted_iota(jnp.int32, shape, 1)
    allowed = (seg_col[start:high, :] == seg_row[0][:, low:high]) & (k_pos <= q_pos)
    scores = jnp.where(allowed, scores, MASKED)
    expo = jnp.exp(scores - jnp.max(scores, axis=1, keepdims=True))
    return expo * (1.0 / jnp.sum(expo, axis=1, keepdims=True)), q, k, start, low, high


def attn_fwd_kernel(block, scale, q_lin, k_lin, v_lin, cosine, sine, seg_row, seg_col, att, rot):
    cos_t = cosine[...]
    sin_t = sine[...]
    for s, lin in ((0, q_lin), (1, k_lin)):
        z = lin[...]
        rot[s] = (z * cos_t + pltpu.roll(z, HEAD_DIM // 2, 1) * sin_t).astype(bf16)
    rot[2] = v_lin[...].astype(bf16)
    for i in range(q_lin.shape[0] // block):
        probs, _, _, start, low, high = block_probs(i, rot, seg_row, seg_col, block, scale)
        att[start:high, :] = dot(probs.astype(bf16), rot[2, low:high, :], NN).astype(bf16)


def attn_bwd_kernel(block, scale, rot, g_att, cosine, sine, seg_row, seg_col, grads, dk, dv):
    cos_t = cosine[...]
    sin_t = sine[...]
    cols = grads.shape[1] // 3
    at = pl.program_id(1) * HEAD_DIM
    dk[...] = jnp.zeros_like(dk)
    dv[...] = jnp.zeros_like(dv)

    def lanes(s):
        return pl.ds(pl.multiple_of(s * cols + at, HEAD_DIM), HEAD_DIM)

    def back(z, c, s):
        return (z * c - pltpu.roll(z, HEAD_DIM // 2, 1) * s).astype(bf16)

    for i in range(rot.shape[1] // block):
        probs, q, k, start, low, high = block_probs(i, rot, seg_row, seg_col, block, scale)
        g = g_att[start:high, :]
        g_probs = dot(g, rot[2, low:high, :], NT)
        delta = jnp.sum(probs * g_probs, axis=1, keepdims=True)
        g_raw = (probs * (g_probs - delta) * scale).astype(bf16)
        grads[start:high, lanes(0)] = back(
            dot(g_raw, k, NN), cos_t[start:high, :], sin_t[start:high, :]
        )
        dk[low:high, :] += dot(g_raw, q, TN)
        dv[low:high, :] += dot(probs.astype(bf16), g, TN)
    grads[:, lanes(1)] = back(dk[...], cos_t, sin_t)
    grads[:, lanes(2)] = dv[...].astype(bf16)


def attention_specs(row_len):
    triple = pl.BlockSpec((3, row_len, HEAD_DIM), lambda r, h: (0, r, h))
    plain = pl.BlockSpec((row_len, HEAD_DIM), lambda r, h: (r, h))
    table = pl.BlockSpec((row_len, HEAD_DIM), lambda r, h: (0, 0))
    seg_row = pl.BlockSpec((1, 1, row_len), lambda r, h: (r, 0, 0))
    seg_col = pl.BlockSpec((row_len, 1), lambda r, h: (r, 0))
    return triple, plain, table, seg_row, seg_col


def attn_forward(lin, cos_t, sin_t, segs, seg_col):
    tokens = lin.shape[0]
    cols = lin.shape[1] // 3
    heads = cols // HEAD_DIM
    rows, row_len = segs.shape
    triple, plain, table, row_spec, col_spec = attention_specs(row_len)
    block = min(QUERY_BLOCK, row_len)
    parts = [
        pl.BlockSpec((row_len, HEAD_DIM), lambda r, h, s=s: (r, s * heads + h)) for s in range(3)
    ]
    return pl.pallas_call(
        functools.partial(attn_fwd_kernel, block, HEAD_DIM**-0.5),
        grid=(rows, heads),
        in_specs=[*parts, table, table, row_spec, col_spec],
        out_specs=[plain, triple],
        out_shape=[
            jax.ShapeDtypeStruct((tokens, cols), bf16),
            jax.ShapeDtypeStruct((3, tokens, cols), bf16),
        ],
        compiler_params=pltpu.CompilerParams(vmem_limit_bytes=VMEM),
        cost_estimate=COST,
    )(lin, lin, lin, cos_t, sin_t, segs[:, None, :], seg_col)


def attn_backward(rot, g_att, cos_t, sin_t, segs, seg_col):
    _, tokens, cols = rot.shape
    rows, row_len = segs.shape
    triple, plain, table, row_spec, col_spec = attention_specs(row_len)
    block = min(QUERY_BLOCK, row_len)
    return pl.pallas_call(
        functools.partial(attn_bwd_kernel, block, HEAD_DIM**-0.5),
        grid=(rows, cols // HEAD_DIM),
        in_specs=[triple, plain, table, table, row_spec, col_spec],
        out_specs=pl.BlockSpec((row_len, 3 * cols), lambda r, h: (r, 0)),
        out_shape=jax.ShapeDtypeStruct((tokens, 3 * cols), bf16),
        scratch_shapes=[pltpu.VMEM((row_len, HEAD_DIM), f32)] * 2,
        compiler_params=pltpu.CompilerParams(vmem_limit_bytes=VMEM),
        cost_estimate=COST,
    )(rot, g_att, cos_t, sin_t, segs[:, None, :], seg_col)


def after(value, *deps):
    return lax.optimization_barrier((value,) + deps)[0]


def join_kernel(n, chunks, *refs):
    per = 2 * n - 1
    out, sem = refs[chunks * per], refs[chunks * per + 1]
    me = lax.axis_index("mp")
    at = 0
    for c in range(chunks):
        own, right, left = refs[c * per], refs[c * per + 1 : c * per + n], refs[c * per + n : c * per + per]
        rows, cols = own.shape

        def put(src, block, at=at, rows=rows, cols=cols):
            target = out.at[
                pl.ds(at, rows), pl.ds(pl.multiple_of(block * cols, cols), cols)
            ]
            pltpu.make_async_copy(src, target, sem).start()

        at += rows
        put(own, me)
        for s in range(1, n):
            pl.when(me >= s)(functools.partial(put, right[s - 1], me - s))
            pl.when(me + s < n)(functools.partial(put, left[s - 1], me + s))
    pltpu.make_async_copy(out, out, sem).wait()


def join(parts):
    n = lax.axis_size("mp")
    rows = sum(p[0].shape[0] for p in parts)
    flat = [a for own, right, left in parts for a in (own, *right, *left)]
    shape = (rows, n * parts[0][0].shape[1])
    return pl.pallas_call(
        functools.partial(join_kernel, n, len(parts)),
        in_specs=[pl.BlockSpec(memory_space=pl.ANY)] * len(flat),
        out_specs=pl.BlockSpec(memory_space=pltpu.VMEM),
        out_shape=jax.ShapeDtypeStruct(shape, parts[0][0].dtype),
        scratch_shapes=[pltpu.SemaphoreType.DMA(())],
        compiler_params=pltpu.CompilerParams(vmem_limit_bytes=VMEM),
        cost_estimate=COST,
    )(*flat)


def line_step(s, right, left):
    n = lax.axis_size("mp")
    return (
        lax.ppermute(right, "mp", [(i, i + 1) for i in range(s - 1, n - 1)]),
        lax.ppermute(left, "mp", [(i, i - 1) for i in range(1, n - s + 1)]),
    )


def line_parts(block, first=None):
    right = left = block
    rights, lefts = [], []
    for s in range(1, lax.axis_size("mp")):
        if s == 1 and first is not None:
            right, left = first
        else:
            right, left = line_step(s, right, left)
        rights.append(right)
        lefts.append(left)
    return block, rights, lefts


def line_gather(chunks):
    return join([line_parts(c) for c in chunks])


def split_rows(x, chunks=2):
    return jnp.split(x, chunks, axis=0)


class Scatter:
    def __init__(self, y):
        self.n = lax.axis_size("mp")
        self.me = lax.axis_index("mp")
        self.y = y
        self.step = 0
        self.x = (self.block(self.n - 1), self.block(1 - self.n))
        self.flight = None
        self.launch()

    def block(self, offset):
        cols = self.y.shape[1] // self.n
        at = jnp.clip(self.me + offset, 0, self.n - 1) * cols
        return lax.dynamic_slice_in_dim(self.y, at, cols, 1)

    def launch(self):
        self.step += 1
        n, s = self.n, self.step
        if s < n:
            right, left = self.x
            self.flight = (
                lax.ppermute(right, "mp", [(i, i + 1) for i in range(s)]),
                lax.ppermute(left, "mp", [(i, i - 1) for i in range(n - s, n)]),
            )

    def land(self):
        if self.flight is not None:
            ahead = self.n - self.step - 1
            self.x = self.flight
            if ahead > 0:
                self.x = tuple(
                    (a.astype(f32) + self.block(offset).astype(f32)).astype(bf16)
                    for a, offset in zip(self.x, (ahead, -ahead))
                )
            self.flight = None

    def finish(self):
        while self.flight is not None:
            self.land()
            self.launch()
        return sum(a.astype(f32) for a in (*self.x, self.block(0)))


def dp_pairs(bits):
    return [(i, i ^ (1 << bits[i & 1])) for i in range(lax.axis_size("dp"))]


def dp_rounds():
    rest = list(range(1, lax.axis_size("dp").bit_length() - 1))
    return list(zip(rest, rest[1:] + rest[:1]))


def by_parity(odd, bits, value):
    return jnp.where(odd == 1, value(bits[1]), value(bits[0]))


class Pieces:
    def __init__(self, piece, place, rounds):
        self.x = (piece,)
        self.flight = None
        self.me = lax.axis_index("dp")
        self.owners = [self.me]
        self.place = place
        self.rounds = list(reversed(rounds))
        self.todo = self.rounds + [(0, 0)]

    def launch(self):
        if self.todo and self.flight is None:
            bits = self.todo.pop(0)
            if self.todo and len(self.x) > 1:
                self.x = (jnp.concatenate(self.x),)
            got = tuple(lax.ppermute(p, "dp", dp_pairs(bits)) for p in self.x)
            self.flight = (bits, got)

    def land(self):
        if self.flight is None:
            return
        bits, got = self.flight
        self.flight = None
        self.x = self.x + got
        if self.todo:
            flip = by_parity(self.me & 1, bits, lambda b: 1 << b)
            self.owners = self.owners + [o ^ flip for o in self.owners]
        else:
            theirs = [self.me ^ 1]
            for bits in self.rounds:
                flip = by_parity(1 - (self.me & 1), bits, lambda b: 1 << b)
                theirs = theirs + [o ^ flip for o in theirs]
            self.owners = self.owners + theirs

    def finish(self, groups=1):
        while self.todo or self.flight is not None:
            self.land()
            self.launch()
        return widen(self.x, jnp.stack([self.place(o) for o in self.owners]), groups)


class Halving:
    def __init__(self, make, whole=False):
        self.me = lax.axis_index("dp")
        odd = self.me & 1
        self.todo = dp_rounds()
        self.whole = whole
        self.pieces = None
        sent = make(1 - odd)
        self.x = (make(after(odd, sent)),)
        self.flight = lax.ppermute(sent, "dp", dp_pairs((0, 0)))

    def place(self, device):
        odd = device & 1
        at = odd
        if not self.whole:
            for bits in dp_rounds():
                at = at * 2 + by_parity(odd, bits, lambda b: (device >> b) & 1)
        return at

    def launch(self):
        if self.pieces is not None:
            self.pieces.x = self.x
            self.pieces.launch()
        elif self.todo and self.flight is None:
            bits = self.todo.pop(0)
            *kept, sent = self.x
            self.x = tuple(kept) or (sent,)
            self.flight = lax.ppermute(sent, "dp", dp_pairs(bits))

    def land(self):
        if self.pieces is not None:
            self.pieces.land()
            self.x = self.pieces.x
        elif self.flight is not None:
            (kept,) = self.x
            got = self.flight
            self.flight = None

            def add(at=0, rows=kept.shape[0]):
                terms = (lax.dynamic_slice_in_dim(a, at, rows, 0) for a in (kept, got))
                return sum(a.astype(f32) for a in terms).astype(bf16)

            if not self.todo:
                self.x = (add(),)
                rounds = [] if self.whole else dp_rounds()
                self.pieces = Pieces(self.x[0], self.place, rounds)
            elif self.whole:
                self.x = (add(),)
            else:
                half = kept.shape[0] // 2
                bit = by_parity(self.me & 1, self.todo[0], lambda b: (self.me >> b) & 1)
                self.x = (add(bit * half, half), add((1 - bit) * half, half))

    def finish(self, groups=1):
        while self.pieces is None:
            self.land()
            self.launch()
        self.pieces.x = self.x
        return self.pieces.finish(groups)


def widen_kernel(firsts, table, *refs):
    *arrays, out = refs
    groups, _, cols = out.shape
    step = pl.program_id(0)
    for k, src in enumerate(arrays):

        @pl.when((step >= firsts[k]) & (step < firsts[k + 1]))
        def _(src=src):
            for g in range(groups):
                out[g] = src[:, g * cols : (g + 1) * cols].astype(f32)


def widen(arrays, places, groups):
    total = sum(a.shape[0] for a in arrays)
    cols = arrays[0].shape[1]
    rows = total // places.shape[0]
    block = min(256, rows)
    per = rows // block
    wide = cols // groups
    firsts = [sum(a.shape[0] for a in arrays[:k]) // block for k in range(len(arrays) + 1)]

    def spec(k):
        def index(step, table):
            return (jnp.clip(step - firsts[k], 0, firsts[k + 1] - firsts[k] - 1), 0)

        return pl.BlockSpec((block, cols), index)

    def out_index(step, table):
        return (0, table[step // per] * per + step % per, 0)

    return pl.pallas_call(
        functools.partial(widen_kernel, firsts),
        grid_spec=pltpu.PrefetchScalarGridSpec(
            num_scalar_prefetch=1,
            grid=(total // block,),
            in_specs=[spec(k) for k in range(len(arrays))],
            out_specs=pl.BlockSpec((groups, block, wide), out_index),
        ),
        out_shape=jax.ShapeDtypeStruct((groups, total, wide), f32),
        compiler_params=pltpu.CompilerParams(vmem_limit_bytes=VMEM),
        cost_estimate=COST,
    )(places.astype(jnp.int32), *arrays)


def half_lanes(x, half):
    size = x.shape[1] // 2
    return lax.dynamic_slice_in_dim(x, half * size, size, 1)


def meet(values, *sums):
    for h in sums:
        h.land()
    met, xs = lax.optimization_barrier((tuple(values), tuple(h.x for h in sums)))
    for h, x in zip(sums, xs):
        h.x = x
        h.launch()
    return met


def butterfly_sum(x, axis):
    size = lax.axis_size(axis)
    for bit in range(size.bit_length() - 1):
        x = x + lax.ppermute(x, axis, [(i, i ^ (1 << bit)) for i in range(size)])
    return x


def norm_qkv_kernel(x, weight, gain, bias, rows, lin):
    v = x[...].astype(f32)
    centred = v - jnp.mean(v, axis=1, keepdims=True)
    rstd = lax.rsqrt(jnp.mean(centred * centred, axis=1, keepdims=True) + EPSILON)
    normed = (centred * rstd * gain[...] + bias[...]).astype(bf16)
    rows[...] = normed
    cols = weight.shape[2]
    for s in range(3):
        lin[:, s * cols : (s + 1) * cols] = dot(normed, weight[s], NN)


def norm_qkv(x, tokens, weight, gain, bias):
    _, width, cols = weight.shape
    block = min(256, tokens)
    rows = pl.BlockSpec((block, width), lambda r: (r, 0))
    vector = pl.BlockSpec((1, width), lambda r: (0, 0))
    return pl.pallas_call(
        norm_qkv_kernel,
        grid=(tokens // block,),
        in_specs=[rows, pl.BlockSpec((3, width, cols), lambda r: (0, 0, 0)), vector, vector],
        out_specs=[rows, pl.BlockSpec((block, 3 * cols), lambda r: (r, 0))],
        out_shape=[
            jax.ShapeDtypeStruct((tokens, width), bf16),
            jax.ShapeDtypeStruct((tokens, 3 * cols), f32),
        ],
        compiler_params=pltpu.CompilerParams(vmem_limit_bytes=VMEM),
        cost_estimate=COST,
    )(x, weight, gain[None], bias[None])


def project_norm_kernel(att, weight, x, gain, bias, mid, rows, held, sem):
    dp_size, mp_size, part, _ = weight.shape

    @pl.when(pl.program_id(0) == 0)
    def _():
        for d in range(dp_size):
            for j in range(mp_size):
                target = held.at[pl.ds((j * dp_size + d) * part, part), :]
                pltpu.make_async_copy(weight.at[d, j], target, sem).start()
        pltpu.make_async_copy(held, held, sem).wait()

    v = x[...].astype(f32) + dot(att[...], held[...], NN)
    mid[...] = v
    centred = v - jnp.mean(v, axis=1, keepdims=True)
    rstd = lax.rsqrt(jnp.mean(centred * centred, axis=1, keepdims=True) + EPSILON)
    rows[...] = (centred * rstd * gain[...] + bias[...]).astype(bf16)


def project_norm(att, weight, x, gain, bias):
    tokens, width = att.shape
    block = min(256, tokens)
    rows = pl.BlockSpec((block, width), lambda r: (r, 0))
    vector = pl.BlockSpec((1, width), lambda r: (0, 0))
    return pl.pallas_call(
        project_norm_kernel,
        grid=(tokens // block,),
        in_specs=[rows, pl.BlockSpec(memory_space=pl.ANY), rows, vector, vector],
        out_specs=[rows, rows],
        out_shape=[
            jax.ShapeDtypeStruct((tokens, width), f32),
            jax.ShapeDtypeStruct((tokens, width), bf16),
        ],
        scratch_shapes=[pltpu.VMEM((width, width), bf16), pltpu.SemaphoreType.DMA(())],
        compiler_params=pltpu.CompilerParams(vmem_limit_bytes=VMEM),
        cost_estimate=COST,
    )(att, weight, x, gain[None], bias[None])


def add_rows(vec, *arrays):
    @pl.when(pl.program_id(0) == 0)
    def _():
        vec[...] = jnp.zeros_like(vec)

    for i, a in enumerate(arrays):
        vec[i : i + 1, :] += jnp.sum(a, axis=0, keepdims=True)


def attn_in_backward_kernel(g, weight, x, gain, low, plain, cross, vec):
    cols = weight.shape[2]
    part = sum(dot(g[:, s * cols : (s + 1) * cols], weight[s], NT) for s in range(3))
    low[...] = part.astype(bf16)
    v = x[...].astype(f32)
    centred = v - jnp.mean(v, axis=1, keepdims=True)
    xhat = centred * lax.rsqrt(jnp.mean(centred * centred, axis=1, keepdims=True) + EPSILON)
    crossed = part * xhat
    plain[...] = jnp.sum(part * gain[...], axis=1, keepdims=True)
    cross[...] = jnp.sum(crossed * gain[...], axis=1, keepdims=True)
    add_rows(vec, crossed, part)


def attn_in_backward(g_rows, weight, x, gain):
    tokens, wide = g_rows.shape
    width, cols = weight.shape[1:]
    block = min(256, tokens)
    rows = pl.BlockSpec((block, width), lambda r: (r, 0))
    column = pl.BlockSpec((block, 1), lambda r: (r, 0))
    return pl.pallas_call(
        attn_in_backward_kernel,
        grid=(tokens // block,),
        in_specs=[
            pl.BlockSpec((block, wide), lambda r: (r, 0)),
            pl.BlockSpec((3, width, cols), lambda r: (0, 0, 0)),
            rows,
            pl.BlockSpec((1, width), lambda r: (0, 0)),
        ],
        out_specs=[rows, column, column, pl.BlockSpec((2, width), lambda r: (0, 0))],
        out_shape=[
            jax.ShapeDtypeStruct((tokens, width), bf16),
            jax.ShapeDtypeStruct((tokens, 1), f32),
            jax.ShapeDtypeStruct((tokens, 1), f32),
            jax.ShapeDtypeStruct((2, width), f32),
        ],
        compiler_params=pltpu.CompilerParams(vmem_limit_bytes=VMEM),
        cost_estimate=COST,
    )(g_rows, weight, x, gain[None])


def mid_backward_kernel(me, g_ffn, gy, mid, gain, low, mine, vec):
    v = mid[...]
    centred = v - jnp.mean(v, axis=1, keepdims=True)
    rstd = lax.rsqrt(jnp.mean(centred * centred, axis=1, keepdims=True) + EPSILON)
    xhat = centred * rstd
    grad_normed = g_ffn[...].astype(f32)
    add_rows(vec, grad_normed * xhat, grad_normed)
    scaled = grad_normed * gain[...]
    plain = jnp.mean(scaled, axis=1, keepdims=True)
    cross = jnp.mean(scaled * xhat, axis=1, keepdims=True)
    grad = gy[...].astype(f32) + rstd * (scaled - plain - xhat * cross)
    low[...] = grad.astype(bf16)
    cols = mine.shape[1]
    for j in range(grad.shape[1] // cols):

        @pl.when(me[0] == j)
        def _(j=j):
            mine[...] = grad[:, j * cols : (j + 1) * cols]


def mid_backward(g_ffn, gy, mid, gain):
    tokens, width = mid.shape
    feats = width // lax.axis_size("mp")
    block = min(128, tokens)
    rows = pl.BlockSpec((block, width), lambda r, me: (r, 0))
    return pl.pallas_call(
        mid_backward_kernel,
        grid_spec=pltpu.PrefetchScalarGridSpec(
            num_scalar_prefetch=1,
            grid=(tokens // block,),
            in_specs=[rows, rows, rows, pl.BlockSpec((1, width), lambda r, me: (0, 0))],
            out_specs=[
                rows,
                pl.BlockSpec((block, feats), lambda r, me: (r, 0)),
                pl.BlockSpec((2, width), lambda r, me: (0, 0)),
            ],
        ),
        out_shape=[
            jax.ShapeDtypeStruct((tokens, width), bf16),
            jax.ShapeDtypeStruct((tokens, feats), f32),
            jax.ShapeDtypeStruct((2, width), f32),
        ],
        compiler_params=pltpu.CompilerParams(vmem_limit_bytes=VMEM),
        cost_estimate=COST,
    )(lax.axis_index("mp").reshape(1).astype(jnp.int32), g_ffn, gy, mid, gain[None])


def split_bits(v):
    high = lax.reduce_precision(v, 8, 7)
    return [high.astype(bf16), (v - high).astype(bf16)]


def normalize(v):
    mean = jnp.mean(v, axis=1, keepdims=True)
    centred = v - mean
    rstd = lax.rsqrt(jnp.mean(centred * centred, axis=1, keepdims=True) + EPSILON)
    return centred * rstd, rstd


def local(
    inputs,
    segment_ids,
    width_bucket,
    attn_gain,
    attn_bias,
    qkv_weight,
    proj_weight,
    ffn_gain,
    ffn_bias,
    up_weight,
    down_weight,
    grad_result,
):
    tokens, feats = inputs.shape
    row_len = segment_ids.shape[1]
    mp_size = lax.axis_size("mp")
    dp_size = lax.axis_size("dp")
    mp_idx = lax.axis_index("mp")
    width = feats * mp_size

    def own(a):
        return lax.dynamic_slice_in_dim(a, mp_idx * feats, feats, a.ndim - 1)

    half = HEAD_DIM // 2
    freqs = jnp.power(10000.0, -jnp.arange(half, dtype=f32) / half)
    angles = jnp.arange(row_len, dtype=f32)[:, None] * freqs[None, :]
    cos_h, sin_h = jnp.cos(angles), jnp.sin(angles)
    cos_t = jnp.concatenate([cos_h, cos_h], axis=1)
    sin_t = jnp.concatenate([-sin_h, sin_h], axis=1)

    vectors = sum((split_bits(v) for v in (attn_gain, attn_bias, ffn_gain, ffn_bias)), [])
    packed = jnp.concatenate([jnp.stack(vectors), jnp.zeros((8, feats), bf16)])
    first, second = split_rows(inputs)
    chunks = [first, jnp.concatenate([second, packed])]
    starts = [line_step(1, c, c) for c in chunks]
    starts[0], cos_t, sin_t, seg_col = lax.optimization_barrier(
        (starts[0], cos_t, sin_t, segment_ids.reshape(tokens, 1))
    )
    parts = [line_parts(c, pair) for c, pair in zip(chunks, starts)]
    gy_own = after(grad_result, *(p[1][min(1, mp_size - 2)] for p in parts))
    gathered = join(parts)
    vec = gathered[tokens : tokens + 8].astype(f32)
    gain_a, bias_a, gain_f, bias_f = (vec[2 * i] + vec[2 * i + 1] for i in range(4))
    gy_steps = [line_step(1, gy_own, gy_own)]

    part = proj_weight.shape[0] // dp_size
    slab = lax.dynamic_slice_in_dim(proj_weight, lax.axis_index("dp") * part, part, 0)
    slab = lax.all_gather(after(slab, gathered), "mp", axis=0)
    attn_rows, lin = norm_qkv(gathered, tokens, qkv_weight, gain_a, bias_a)
    att, rot = attn_forward(lin, cos_t, sin_t, segment_ids, seg_col)
    att, slab, gy_steps[0] = lax.optimization_barrier((att, slab, gy_steps[0]))
    proj_full = lax.all_gather(slab, "dp", axis=0)
    att_full, proj_full = lax.optimization_barrier((line_gather(split_rows(att)), proj_full))
    gy_steps[0] = tuple(after(a, att_full) for a in gy_steps[0])
    gy_steps.append(line_step(2, *gy_steps[0]))
    mid, ffn_rows = project_norm(att_full, proj_full, gathered, gain_f, bias_f)
    ffn_rows, gy_steps[1] = lax.optimization_barrier((ffn_rows, gy_steps[1]))
    for s in range(3, mp_size):
        gy_steps.append(line_step(s, *gy_steps[-1]))

    limit = (width_bucket.reshape(tokens) + 1) * (FF // 4)
    columns = mp_idx * up_weight.shape[1] + jnp.arange(up_weight.shape[1], dtype=jnp.int32)
    keep = columns[None, :] < limit[:, None]
    hidden = dot(ffn_rows, up_weight, NN)
    relu = jnp.where(keep, jnp.maximum(hidden, 0.0), 0.0)
    active = (relu * relu).astype(bf16)

    gy = join([(gy_own, [r for r, _ in gy_steps], [l for _, l in gy_steps])])
    gy, active, relu = lax.optimization_barrier((gy, active, relu))
    grad_hidden = (2.0 * relu * dot(gy, down_weight, NT)).astype(bf16)
    g_ffn_part = dot(grad_hidden, up_weight, NT).astype(bf16)
    g_ffn_own = lax.psum_scatter(g_ffn_part, "mp", scatter_dimension=1, tiled=True)

    active, gy = (after(a, g_ffn_part) for a in (active, gy))
    down = Halving(lambda half: dot(half_lanes(active, half), gy, TN).astype(bf16))
    grad_up = dot(after(ffn_rows, down.x), grad_hidden, TN).astype(bf16)
    (grad_up,) = meet((grad_up,), down)
    grad_up = lax.psum_scatter(grad_up, "dp", scatter_dimension=0, tiled=True)
    ffn_part = dot(after(active, down.x), down_weight, NN).astype(bf16)
    down.x = after(down.x, ffn_part)
    g_ffn_own, ffn_part = meet((g_ffn_own, ffn_part), down)
    chunks = split_rows(g_ffn_own)
    starts = [line_step(1, c, c) for c in chunks]
    starts[0] = meet(starts[0], down)
    g_ffn = join([line_parts(c, pair) for c, pair in zip(chunks, starts)])
    up = Pieces(grad_up, lambda device: device, dp_rounds())
    g_ffn, ffn_part = meet((g_ffn, ffn_part), up, down)
    ffn_out = lax.psum_scatter(ffn_part, "mp", scatter_dimension=1, tiled=True)

    grad_mid_low, grad_mid_own, ffn_vec = mid_backward(g_ffn, gy, mid, gain_f)
    g_att = dot(grad_mid_low, proj_weight, NT).astype(bf16)
    g_qkv_rows = attn_backward(rot, g_att, cos_t, sin_t, segment_ids, seg_col)
    (g_qkv_rows,) = meet((g_qkv_rows,), down)
    qkv = Halving(lambda half: dot(half_lanes(attn_rows, half), g_qkv_rows, TN).astype(bf16))
    (later,) = meet((g_qkv_rows,), qkv, up)
    g_attn_low, plain, cross, attn_vec = attn_in_backward(later, qkv_weight, gathered, gain_a)
    g_attn = lax.psum_scatter(g_attn_low, "mp", scatter_dimension=1, tiled=True).astype(f32)

    mid_later, _, ffn_out = meet((grad_mid_low, g_attn_low, ffn_out), down)
    made = []

    def make_proj(half):
        rows = mid_later
        if made:
            rows, _ = meet((mid_later, made[0]), qkv)
        made.append(dot(half_lanes(att, half), rows, TN).astype(bf16))
        return made[-1]

    proj = Halving(make_proj)
    (down.x,) = meet((after(down.x, proj.x),), qkv, proj, up)
    (grad_down,) = meet((down.finish()[0],), qkv, proj)
    up.x = after(up.x, grad_down)
    (grad_up,) = meet((up.finish()[0],), qkv, proj)
    sums = jnp.concatenate([attn_vec, jnp.stack([plain, cross]).reshape(-1, width)])
    sums = butterfly_sum(sums, "mp")
    sum_plain, sum_cross = sums[2:].reshape(2, tokens, 1)
    vec = jnp.concatenate([own(sums[:2]), own(ffn_vec)])
    vec, sum_plain, g_attn = meet((vec, sum_plain, g_attn), qkv, proj)
    grad_vec = butterfly_sum(vec, "dp")
    grad_qkv, grad_proj = qkv.finish(3), proj.finish()[0]

    ffn_out = ffn_out.astype(f32)
    xhat_a, rstd_a = normalize(after(gathered, grad_up)[:tokens].astype(f32))
    grad_input = grad_mid_own + rstd_a * (
        g_attn * attn_gain - sum_plain / width - own(xhat_a) * (sum_cross / width)
    )
    block_output = (own(mid) + ffn_out).astype(bf16)
    return (
        block_output,
        grad_input,
        grad_vec[0],
        grad_vec[1],
        grad_qkv,
        grad_proj,
        grad_vec[2],
        grad_vec[3],
        grad_up,
        grad_down,
    )


def solution(mesh):
    placed = (
        P("dp", "mp"),
        P("dp", None),
        P("dp", None),
        P("mp"),
        P("mp"),
        P(None, None, "mp"),
        P("mp", None),
        P("mp"),
        P("mp"),
        P(None, "mp"),
        P("mp", None),
        P("dp", "mp"),
    )
    return jax.shard_map(
        local,
        mesh=mesh,
        in_specs=placed,
        out_specs=(
            P("dp", "mp"),
            P("dp", "mp"),
            P("mp"),
            P("mp"),
            P(None, None, "mp"),
            P("mp", None),
            P("mp"),
            P("mp"),
            P(None, "mp"),
            P("mp", None),
        ),
        check_vma=False,
    )
```
